32 devices in a mesh: node: 4 (over x, core), head: 8 (over z, y).
Axes of the slice: x: 2, y: 2, z: 4, core: 2. Of those that a mesh axis runs over, the one named last changes fastest.
Arguments:
- node_feats: bfloat16 [1024, 4096], P('node', 'head'), may hold values from -6 to 6
- w_qk: bfloat16 [4096, 4096], P('node', 'head'), may hold values from -0.09375 to 0.09375
- w_val: bfloat16 [4096, 4096], P('node', 'head'), may hold values from -0.09375 to 0.09375
- w_out: bfloat16 [4096, 4096], P('head', 'node'), may hold values from -0.75 to 0.75
- edge_types: int32 [8, 8], P('node'), may hold values from 0 to 236
- rel_bias: float32 [237, 32], P(None, 'head'), may hold values from -8 to 300
Outputs:
- mixed: bfloat16 [1024, 4096], P('node', 'head')
The draws below stay inside these ranges and needn't reach their ends.
All inputs are finite; a program needn't handle non-finite values.
Results may differ from the reference program's by a relative error of at most 0.018.
Values may be sent and summed in bfloat16 or wider, within the bound.
No kernel may reach another device: no remote copies, remote signals or barrier semaphores. Data moves between devices by JAX's collectives and lax.ppermute only.
A program may use at most 64 MiB of HBM per device.

```python
import jax
import jax.numpy as jnp
from jax import lax

D = 4096
H = 32
DH = 128
TILE = 128
RELS = 237
NODES = 1024
NT = 8
N_HEAD = 8


def draw_rel_bias(key, part):
    key = jax.random.fold_in(key, 11)
    first_key = jax.random.fold_in(key, 0)
    return jnp.clip(jax.random.normal(first_key, (RELS, H), jnp.float32) * 2.5, -8.0, 8.0)


def plant(entries, rng, smallest, top_value):
    place = [jax.random.randint(jax.random.fold_in(rng, axis), (), 0, length) for axis, length in enumerate(entries.shape)]
    main_axis = entries.shape.index(max(entries.shape))
    neighbour = place[:main_axis] + [(place[main_axis] + 1) % entries.shape[main_axis]] + place[main_axis + 1:]
    return entries.at[tuple(place)].set(smallest).at[tuple(neighbour)].set(top_value)


def level_of(key, dims, shards, low, top_value):
    level, own = 1.0, jax.random.fold_in(key, 6)
    for dim, blocks in shards:
        steps = jnp.exp(jax.random.uniform(jax.random.fold_in(own, dim), (blocks,), jnp.float32, low / len(shards), top_value / len(shards)))
        level = level * jnp.repeat(steps, dims[dim] // blocks).reshape([-1 if axis == dim else 1 for axis in range(len(dims))])
    return level


def noise(rng, extent, deviation, limit, pieces=(), kind=jnp.bfloat16):
    loudness = level_of(rng, extent, pieces, -0.22, 0.18) if pieces else 1.0
    values = jax.random.normal(rng, extent, jnp.float32) * deviation * loudness
    return jnp.minimum(jnp.maximum(values, -limit), limit).astype(kind)


def setup_inputs(seed: int = 0) -> dict:
    key_list = jax.random.split(jax.random.key(seed), 7)
    return {
        "node_feats": noise(key_list[0], (NODES, D), 1.0, 6.0, ((0, 4), (1, 8))),
        "w_qk": noise(key_list[1], (D, H * DH), D ** -0.5, 0.09375, ((0, 4), (1, 8))),
        "w_val": noise(key_list[2], (D, H * DH), D ** -0.5, 0.09375, ((0, 4), (1, 8))),
        "w_out": noise(key_list[3], (H * DH, D), (H * DH // 64) ** -0.5, 0.75, ((0, 8), (1, 4))),
        "edge_types": plant(jax.random.randint(key_list[4], (NT, NT), 0, RELS), jax.random.fold_in(key_list[4], 1), 0, RELS - 1).astype(jnp.int32),
        "rel_bias": draw_rel_bias(jax.random.fold_in(key_list[6], 71), 0),
    }


NEG_BIG = -1.0e30


def reference(node_feats, w_qk, w_val, w_out, edge_types, rel_bias):
    qk_all = jnp.dot(node_feats, w_qk, preferred_element_type=jnp.float32).astype(jnp.bfloat16)
    val_all = jnp.dot(node_feats, w_val, preferred_element_type=jnp.float32).astype(jnp.bfloat16)
    tile_bias = rel_bias[edge_types]
    inv_root = 1.0 / (DH ** 0.5)
    qk_heads = qk_all.reshape(NODES, H, DH).transpose(1, 0, 2)
    val_heads = val_all.reshape(NODES, H, DH).transpose(1, 0, 2)
    bias_heads = tile_bias.transpose(2, 0, 1)
    col_ids = jnp.arange(NODES, dtype=jnp.int32)

    def one_head(packed):
        queries, values, head_bias = packed

        def one_tile(tile_no):
            row_block = lax.dynamic_slice_in_dim(queries, tile_no * TILE, TILE, 0)
            scaled = jnp.dot(row_block, queries.T, preferred_element_type=jnp.float32) * inv_root
            bias_row = lax.dynamic_index_in_dim(head_bias, tile_no, 0, keepdims=False)
            biased = scaled + jnp.repeat(bias_row, TILE, total_repeat_length=NODES)[None, :]
            row_ids = tile_no * TILE + jnp.arange(TILE, dtype=jnp.int32)
            self_mask = row_ids[:, None] == col_ids[None, :]
            biased = jnp.where(self_mask, NEG_BIG, biased)
            top_val = jnp.max(biased, axis=1, keepdims=True)
            expd = jnp.where(self_mask, 0.0, jnp.exp(biased - top_val))
            totals = jnp.sum(expd, axis=1, keepdims=True)
            result = jnp.dot(expd.astype(jnp.bfloat16), values, preferred_element_type=jnp.float32) / totals
            return result.astype(jnp.bfloat16)

        tiles_out = lax.map(one_tile, jnp.arange(NT, dtype=jnp.int32))
        return tiles_out.reshape(NODES, DH)

    heads_out = lax.map(one_head, (qk_heads, val_heads, bias_heads))
    attn = heads_out.transpose(1, 0, 2).reshape(NODES, H * DH)
    group_cols = H * DH // N_HEAD
    attn_groups = attn.reshape(NODES, N_HEAD, group_cols).transpose(1, 0, 2)
    weight_groups = w_out.reshape(N_HEAD, group_cols, D)

    def add_group(running, packed):
        attn_part, weight_part = packed
        product = jnp.dot(attn_part, weight_part, preferred_element_type=jnp.float32).astype(jnp.bfloat16)
        product = lax.optimization_barrier(product)
        return running + product.astype(jnp.float32), None

    summed, _ = lax.scan(add_group, jnp.zeros((NODES, D), jnp.float32), (attn_groups, weight_groups))
    return summed.astype(jnp.bfloat16)
```

```python
import functools

import jax
import jax.numpy as jnp
from jax import lax
from jax.experimental import pallas as pl
from jax.experimental.pallas import tpu as pltpu
from jax.sharding import PartitionSpec as P

DH = 128
TILE = 128


NEG_BIG = -1e30


def swap(value, axis, mask):
    peers = lax.axis_size(axis)
    return lax.ppermute(value, axis, [(i, i ^ mask) for i in range(peers)])


def after(value, *others):
    return lax.optimization_barrier((value, *others))[0]


def vmem_spec():
    return pl.BlockSpec(memory_space=pltpu.VMEM)


def smem_spec():
    return pl.BlockSpec(memory_space=pltpu.SMEM)


def any_spec():
    return pl.BlockSpec(memory_space=pl.ANY)


def project_kernel(place_ref, *refs):
    pieces, weights, outs = refs[:8], refs[8:12], refs[12:16]
    feats, held, total, heads, piece_sem, weight_sem = refs[16:]
    node, head = place_ref[0], place_ref[1]
    copies = []
    for i in range(8):
        copy = pltpu.make_async_copy(pieces[i], feats.at[head ^ i], piece_sem.at[i])
        copy.start()
        copies.append(copy)
    weight_copies = []
    for i in range(4):
        copy = pltpu.make_async_copy(weights[i], held.at[i], weight_sem.at[i])
        copy.start()
        weight_copies.append(copy)
    for copy in copies:
        copy.wait()
    depth = feats.shape[2]
    for i in range(4):
        weight_copies[i].wait()
        for part in range(2):
            term = jnp.dot(
                feats[2 * (node ^ i) + part],
                held[i, part * depth : (part + 1) * depth, :],
                preferred_element_type=jnp.float32,
            )
            if i == 0 and part == 0:
                total[...] = term
            else:
                total[...] += term
    for i in range(4):
        heads[i] = total[:, i * DH : (i + 1) * DH].astype(jnp.bfloat16)
    for i in range(4):
        outs[i][...] = heads[node ^ i]


def project(place, pieces, weights):
    rows, depth = pieces[0].shape
    cols = weights[0].shape[1]
    flops = 2 * rows * 8 * depth * cols
    moved = 2 * (8 * rows * depth + 8 * depth * cols + rows * cols)
    return pl.pallas_call(
        project_kernel,
        out_shape=[jax.ShapeDtypeStruct((rows, DH), jnp.bfloat16)] * 4,
        in_specs=[smem_spec()] + [any_spec()] * 12,
        out_specs=[vmem_spec()] * 4,
        scratch_shapes=[
            pltpu.VMEM((8, rows, depth), jnp.bfloat16),
            pltpu.VMEM((4, 2 * depth, cols), jnp.bfloat16),
            pltpu.VMEM((rows, cols), jnp.float32),
            pltpu.VMEM((4, rows, DH), jnp.bfloat16),
            pltpu.SemaphoreType.DMA((8,)),
            pltpu.SemaphoreType.DMA((4,)),
        ],
        compiler_params=pltpu.CompilerParams(vmem_limit_bytes=20 * 2**20),
        cost_estimate=pl.CostEstimate(flops=flops, bytes_accessed=moved, transcendentals=0),
        name="project",
    )(place, *pieces, *weights)


def attend_kernel(place_ref, edge_ref, bias_ref, *refs):
    queries, values, outs = refs[:4], refs[4:8], refs[8:12]
    node = place_ref[0]
    inv_root = 1.0 / DH**0.5
    rows = queries[0].shape[0]
    tiles = rows // TILE
    for i in range(4):
        for ti in range(tiles):
            mine = queries[i][ti * TILE : (ti + 1) * TILE, :]
            row_tile = tiles * (node ^ i) + ti
            scores = []
            for j in range(4):
                raw = lax.dot_general(
                    mine, queries[j][...], (((1,), (1,)), ((), ())),
                    preferred_element_type=jnp.float32,
                )
                for tj in range(tiles):
                    relation = edge_ref[row_tile, tiles * (node ^ j) + tj]
                    part = raw[:, tj * TILE : (tj + 1) * TILE] * inv_root + bias_ref[relation]
                    if i == j and ti == tj:
                        row_ids = lax.broadcasted_iota(jnp.int32, (TILE, TILE), 0)
                        col_ids = lax.broadcasted_iota(jnp.int32, (TILE, TILE), 1)
                        part = jnp.where(row_ids == col_ids, NEG_BIG, part)
                    scores.append(part)
            top = functools.reduce(jnp.maximum, scores)
            top = jnp.max(top, axis=1, keepdims=True)
            expd = [jnp.exp(part - top) for part in scores]
            total = jnp.sum(functools.reduce(jnp.add, expd), axis=1, keepdims=True)
            mixed = None
            for j in range(4):
                block = jnp.concatenate(
                    [part.astype(jnp.bfloat16) for part in expd[tiles * j : tiles * (j + 1)]], axis=1
                )
                term = jnp.dot(block, values[j][...], preferred_element_type=jnp.float32)
                mixed = term if mixed is None else mixed + term
            outs[i][ti * TILE : (ti + 1) * TILE, :] = (mixed / total).astype(jnp.bfloat16)


def attend(place, edges, bias, queries, values):
    rows = queries[0].shape[0]
    nodes = 4 * rows
    return pl.pallas_call(
        attend_kernel,
        out_shape=[jax.ShapeDtypeStruct((rows, DH), jnp.bfloat16)] * 4,
        in_specs=[smem_spec()] * 3 + [vmem_spec()] * 8,
        out_specs=[vmem_spec()] * 4,
        compiler_params=pltpu.CompilerParams(vmem_limit_bytes=16 * 2**20),
        cost_estimate=pl.CostEstimate(
            flops=4 * nodes * nodes * DH, bytes_accessed=6 * nodes * DH, transcendentals=nodes * nodes
        ),
        name="attend",
    )(place, edges, bias, *queries, *values)


def emit_kernel(place_ref, *refs):
    parts, weights, outs = refs[:4], refs[4:8], refs[8:16]
    held, heads, weight_sem = refs[16:]
    node, head = place_ref[0], place_ref[1]
    far, near = head // 2, head % 2
    copies = []
    for i in range(4):
        copy = pltpu.make_async_copy(weights[i], held.at[node ^ i], weight_sem.at[i])
        copy.start()
        copies.append(copy)
    for i in range(4):
        heads[node ^ i] = parts[i][...]
    attn = jnp.concatenate([heads[i] for i in range(4)], axis=1)
    for copy in copies:
        copy.wait()
    width = outs[0].shape[1]
    for i in (3, 2, 1, 0):
        for side in range(2):
            start = pl.multiple_of((near ^ side) * width, width)
            term = jnp.dot(
                attn, held[far ^ i, :, pl.ds(start, width)], preferred_element_type=jnp.float32
            )
            outs[4 * side + i][...] = term.astype(jnp.bfloat16)


def emit(place, parts, weights):
    rows = parts[0].shape[0]
    depth, cols = weights[0].shape
    flops = 2 * rows * depth * 4 * cols
    moved = 2 * (rows * depth + 4 * depth * cols + 4 * rows * cols)
    return pl.pallas_call(
        emit_kernel,
        out_shape=[jax.ShapeDtypeStruct((rows, cols // 2), jnp.bfloat16)] * 8,
        in_specs=[smem_spec()] + [vmem_spec()] * 4 + [any_spec()] * 4,
        out_specs=[vmem_spec()] * 8,
        scratch_shapes=[
            pltpu.VMEM((4, depth, cols), jnp.bfloat16),
            pltpu.VMEM((4, rows, DH), jnp.bfloat16),
            pltpu.SemaphoreType.DMA((4,)),
        ],
        compiler_params=pltpu.CompilerParams(vmem_limit_bytes=20 * 2**20),
        cost_estimate=pl.CostEstimate(flops=flops, bytes_accessed=moved, transcendentals=0),
        name="emit",
    )(place, *parts, *weights)


def gather_pairs(value):
    across = swap(value, "node", 2)
    beside = swap(value, "node", 1)
    return [value, beside, across, swap(across, "node", 1)]


def exchange_heads(pieces):
    return [pieces[0]] + [swap(pieces[i], "node", i) for i in range(1, 4)]


def one_head_each(node_feats, w_qk, w_val, w_out, edge_types, rel_bias):
    node, head = lax.axis_index("node"), lax.axis_index("head")
    place = jnp.stack([node, head]).astype(jnp.int32)
    edges = lax.all_gather(edge_types, "node", axis=0, tiled=True)
    bias = lax.dynamic_index_in_dim(rel_bias, node, 1, keepdims=False)

    far = {i: swap(node_feats, "head", 2 * i) for i in (3, 2, 1)}
    far[0] = node_feats
    full_qk = gather_pairs(w_qk)
    pieces = [None] * 8
    for i in (0, 1, 2, 3):
        pieces[2 * i] = far[i]
        pieces[2 * i + 1] = swap(far[i], "head", 1)
    full_val = gather_pairs(after(w_val, full_qk[2]))
    full_out = gather_pairs(after(w_out, full_val[2]))

    queries = exchange_heads(project(place, pieces, full_qk))
    values = exchange_heads(project(place, pieces, full_val))
    attn = exchange_heads(attend(place, edges, bias, queries, values))
    terms = emit(place, attn, full_out)
    sums = [None] * 4
    for i in (3, 2, 1, 0):
        near = swap(terms[4 + i], "head", 1)
        sums[i] = terms[i].astype(jnp.float32) + near.astype(jnp.float32)
    total = sums[0]
    for i in (3, 2, 1):
        moved = swap(sums[i].astype(jnp.bfloat16), "head", 2 * i)
        total = total + moved.astype(jnp.float32)
    return total.astype(jnp.bfloat16)


def from_behind(value, axis, by):
    peers = lax.axis_size(axis)
    return lax.ppermute(value, axis, [(i, (i + by) % peers) for i in range(peers)])


def pair_scores(queries, key_rows):
    inv_root = 1.0 / DH**0.5
    return (
        jnp.einsum("qhd,khd->hqk", queries, key_rows, preferred_element_type=jnp.float32) * inv_root
    )


def update(carried, scaled, bias_cols, value_rows, self_mask):
    head_count, query_count, key_count = scaled.shape
    tiles = bias_cols.shape[1]
    biased = (
        scaled.reshape(head_count, tiles, query_count // tiles, key_count)
        + bias_cols[:, :, None, :]
    )
    biased = biased.reshape(head_count, query_count, key_count)
    if self_mask is not None:
        biased = jnp.where(self_mask[None], NEG_BIG, biased)
    top_old, total_old, accum_old = carried
    top_new = jnp.maximum(top_old, jnp.max(biased, axis=2))
    expd = jnp.exp(biased - top_new[:, :, None])
    if self_mask is not None:
        expd = jnp.where(self_mask[None], 0.0, expd)
    factor = jnp.exp(top_old - top_new)
    total_new = total_old * factor + jnp.sum(expd, axis=2)
    product = jnp.einsum(
        "hqk,khd->hqd", expd.astype(jnp.bfloat16), value_rows, preferred_element_type=jnp.float32
    )
    return (top_new, total_new, accum_old * factor[:, :, None] + product)


def on_device(node_feats, w_qk, w_val, w_out, edge_types, rel_bias):
    row_count = node_feats.shape[0]
    col_width = w_qk.shape[1]
    head_count = rel_bias.shape[1]
    tile_rows = edge_types.shape[0]
    full_qk, full_val = (
        lax.all_gather(w_qk, "node", axis=0, tiled=True),
        lax.all_gather(w_val, "node", axis=0, tiled=True),
    )
    shard_piece = lax.all_gather(node_feats, "head", axis=1, tiled=True)
    proj_qk = jnp.dot(shard_piece, full_qk, preferred_element_type=jnp.float32)
    proj_val = jnp.dot(shard_piece, full_val, preferred_element_type=jnp.float32)
    qk_local = proj_qk.astype(jnp.bfloat16)
    val_local = proj_val.astype(jnp.bfloat16)
    queries = qk_local.reshape(row_count, head_count, DH)
    values = val_local.reshape(row_count, head_count, DH)
    relation_ids = jnp.arange(rel_bias.shape[0], dtype=jnp.int32)
    one_hot = (edge_types[:, :, None] == relation_ids[None, None, :]).astype(jnp.float32)
    tile_bias = jnp.einsum("abr,rh->hab", one_hot, rel_bias, precision=lax.Precision.HIGHEST)
    expanded = jnp.repeat(tile_bias, TILE, axis=2)
    my_block = lax.axis_index("node")
    first_row = my_block * row_count
    row_ids = first_row + jnp.arange(row_count, dtype=jnp.int32)
    initial = (
        jnp.full((head_count, row_count), NEG_BIG, jnp.float32),
        jnp.zeros((head_count, row_count), jnp.float32),
        jnp.zeros((head_count, row_count, DH), jnp.float32),
    )
    node_count = lax.axis_size("node")
    rounds = node_count // 2
    own_cols = lax.dynamic_slice_in_dim(expanded, first_row, row_count, 2)
    own_mask = row_ids[:, None] == row_ids[None, :]
    own_state = update(initial, pair_scores(queries, queries), own_cols, values, own_mask)

    def one_round(round_no, carried):
        mine, moving_block, moving_state = carried
        key_flat, value_flat = from_behind((moving_block[0], moving_block[1]), "node", 1)
        bias_moved, top_moved, total_moved, accum_moved = (
            from_behind(moving_state[0].astype(jnp.bfloat16), "node", 1).astype(jnp.float32),
            from_behind(moving_state[1].astype(jnp.bfloat16), "node", 1).astype(jnp.float32),
            from_behind(moving_state[2].astype(jnp.bfloat16), "node", 1).astype(jnp.float32),
            from_behind(moving_state[3].astype(jnp.bfloat16), "node", 1).astype(jnp.float32),
        )
        partner = (my_block - round_no) % node_count
        key_rows = key_flat.reshape(row_count, head_count, DH)
        value_rows = value_flat.reshape(row_count, head_count, DH)
        raw_scores = pair_scores(queries, key_rows)
        mine_cols = lax.dynamic_slice_in_dim(expanded, partner * row_count, row_count, 2)
        mine = update(mine, raw_scores, mine_cols, value_rows, None)
        back_tiles = lax.dynamic_slice_in_dim(bias_moved, my_block * tile_rows, tile_rows, 2)
        back_cols = jnp.repeat(back_tiles, TILE, axis=2)
        passed = update(
            (top_moved, total_moved, accum_moved),
            jnp.transpose(raw_scores, (0, 2, 1)),
            back_cols,
            values,
            None,
        )
        keep_flag = 2 * round_no != node_count
        kept = jax.tree.map(
            lambda fresh, stale: jnp.where(keep_flag, fresh, stale),
            passed,
            (top_moved, total_moved, accum_moved),
        )
        return (mine, (key_flat, value_flat), (bias_moved, kept[0], kept[1], kept[2]))

    start_state = (tile_bias, initial[0], initial[1], initial[2])
    own_state, _, final_moving = lax.fori_loop(
        1, rounds + 1, one_round, (own_state, (qk_local, val_local), start_state)
    )
    top_home, total_home, accum_home = (
        from_behind(final_moving[1].astype(jnp.bfloat16), "node", -rounds).astype(jnp.float32),
        from_behind(final_moving[2].astype(jnp.bfloat16), "node", -rounds).astype(jnp.float32),
        from_behind(final_moving[3].astype(jnp.bfloat16), "node", -rounds).astype(jnp.float32),
    )
    top_fin = jnp.maximum(own_state[0], top_home)
    factor_own = jnp.exp(own_state[0] - top_fin)
    factor_home = jnp.exp(top_home - top_fin)
    total_fin = own_state[1] * factor_own + total_home * factor_home
    accum_fin = own_state[2] * factor_own[:, :, None] + accum_home * factor_home[:, :, None]
    attn_heads = (accum_fin / total_fin[:, :, None]).astype(jnp.bfloat16)
    attn = jnp.transpose(attn_heads, (1, 0, 2)).reshape(row_count, col_width)
    terms = jnp.dot(
        attn, lax.all_gather(w_out, "node", axis=1, tiled=True), preferred_element_type=jnp.float32
    )
    return lax.psum_scatter(terms.astype(jnp.bfloat16), "head", scatter_dimension=1, tiled=True)

def solution(mesh):
    in_specs = (
        P("node", "head"),
        P("node", "head"),
        P("node", "head"),
        P("head", "node"),
        P("node", None),
        P(None, "head"),
    )
    out_specs = P("node", "head")

    def whole(node_feats, w_qk, w_val, w_out, edge_types, rel_bias):
        node_count, head_count = mesh.shape["node"], mesh.shape["head"]
        column_heads = rel_bias.shape[1] // head_count
        fits = (
            node_count == 4
            and head_count == 2 * node_count
            and column_heads == node_count
            and node_feats.shape[0] % (node_count * TILE) == 0
        )
        body = one_head_each if fits else on_device
        mapped = jax.shard_map(
            body, mesh=mesh, in_specs=in_specs, out_specs=out_specs, check_vma=False
        )
        return mapped(node_feats, w_qk, w_val, w_out, edge_types, rel_bias)

    return whole
```

```python
import functools

import jax
import jax.numpy as jnp
from jax import lax
from jax.experimental import pallas as pl
from jax.experimental.pallas import tpu as pltpu
from jax.sharding import PartitionSpec as P

DH = 128
TILE = 128


NEG_BIG = -1e30


def swap(value, axis, mask):
    peers = lax.axis_size(axis)
    return lax.ppermute(value, axis, [(i, i ^ mask) for i in range(peers)])


def after(value, *others):
    return lax.optimization_barrier((value, *others))[0]


def vmem_spec():
    return pl.BlockSpec(memory_space=pltpu.VMEM)


def smem_spec():
    return pl.BlockSpec(memory_space=pltpu.SMEM)


def hbm_spec():
    return pl.BlockSpec(memory_space=pltpu.HBM)


def project_kernel(place_ref, *refs):
    pieces, weights, outs = refs[:8], refs[8:12], refs[12:16]
    feats, held, total, heads, piece_sem, weight_sem = refs[16:]
    node, head = place_ref[0], place_ref[1]
    copies = []
    for i in range(8):
        copy = pltpu.make_async_copy(pieces[i], feats.at[head ^ i], piece_sem.at[i])
        copy.start()
        copies.append(copy)
    weight_copies = []
    for i in range(4):
        copy = pltpu.make_async_copy(weights[i], held.at[i], weight_sem.at[i])
        copy.start()
        weight_copies.append(copy)
    for copy in copies:
        copy.wait()
    depth = feats.shape[2]
    for i in range(4):
        weight_copies[i].wait()
        for part in range(2):
            term = jnp.dot(
                feats[2 * (node ^ i) + part],
                held[i, part * depth : (part + 1) * depth, :],
                preferred_element_type=jnp.float32,
            )
            if i == 0 and part == 0:
                total[...] = term
            else:
                total[...] += term
    for i in range(4):
        heads[i] = total[:, i * DH : (i + 1) * DH].astype(jnp.bfloat16)
    for i in range(4):
        outs[i][...] = heads[node ^ i]


def project(place, pieces, weights):
    rows, depth = pieces[0].shape
    cols = weights[0].shape[1]
    flops = 2 * rows * 8 * depth * cols
    moved = 2 * (8 * rows * depth + 8 * depth * cols + rows * cols)
    return pl.pallas_call(
        project_kernel,
        out_shape=[jax.ShapeDtypeStruct((rows, DH), jnp.bfloat16)] * 4,
        in_specs=[smem_spec()] + [hbm_spec()] * 12,
        out_specs=[vmem_spec()] * 4,
        scratch_shapes=[
            pltpu.VMEM((8, rows, depth), jnp.bfloat16),
            pltpu.VMEM((4, 2 * depth, cols), jnp.bfloat16),
            pltpu.VMEM((rows, cols), jnp.float32),
            pltpu.VMEM((4, rows, DH), jnp.bfloat16),
            pltpu.SemaphoreType.DMA((8,)),
            pltpu.SemaphoreType.DMA((4,)),
        ],
        compiler_params=pltpu.CompilerParams(vmem_limit_bytes=20 * 2**20),
        cost_estimate=pl.CostEstimate(flops=flops, bytes_accessed=moved, transcendentals=0),
        name="project",
    )(place, *pieces, *weights)


def attend_kernel(place_ref, edge_ref, bias_ref, *refs):
    queries, values, outs = refs[:4], refs[4:8], refs[8:12]
    node = place_ref[0]
    inv_root = 1.0 / DH**0.5
    rows = queries[0].shape[0]
    tiles = rows // TILE
    for i in range(4):
        for ti in range(tiles):
            mine = queries[i][ti * TILE : (ti + 1) * TILE, :]
            row_tile = tiles * (node ^ i) + ti
            scores = []
            for j in range(4):
                raw = lax.dot_general(
                    mine, queries[j][...], (((1,), (1,)), ((), ())),
                    preferred_element_type=jnp.float32,
                )
                for tj in range(tiles):
                    relation = edge_ref[row_tile, tiles * (node ^ j) + tj]
                    part = raw[:, tj * TILE : (tj + 1) * TILE] * inv_root + bias_ref[relation]
                    if i == j and ti == tj:
                        row_ids = lax.broadcasted_iota(jnp.int32, (TILE, TILE), 0)
                        col_ids = lax.broadcasted_iota(jnp.int32, (TILE, TILE), 1)
                        part = jnp.where(row_ids == col_ids, NEG_BIG, part)
                    scores.append(part)
            top = functools.reduce(jnp.maximum, scores)
            top = jnp.max(top, axis=1, keepdims=True)
            expd = [jnp.exp(part - top) for part in scores]
            total = jnp.sum(functools.reduce(jnp.add, expd), axis=1, keepdims=True)
            mixed = None
            for j in range(4):
                block = jnp.concatenate(
                    [part.astype(jnp.bfloat16) for part in expd[tiles * j : tiles * (j + 1)]], axis=1
                )
                term = jnp.dot(block, values[j][...], preferred_element_type=jnp.float32)
                mixed = term if mixed is None else mixed + term
            outs[i][ti * TILE : (ti + 1) * TILE, :] = (mixed / total).astype(jnp.bfloat16)


def attend(place, edges, bias, queries, values):
    rows = queries[0].shape[0]
    nodes = 4 * rows
    return pl.pallas_call(
        attend_kernel,
        out_shape=[jax.ShapeDtypeStruct((rows, DH), jnp.bfloat16)] * 4,
        in_specs=[smem_spec()] * 3 + [vmem_spec()] * 8,
        out_specs=[vmem_spec()] * 4,
        compiler_params=pltpu.CompilerParams(vmem_limit_bytes=16 * 2**20),
        cost_estimate=pl.CostEstimate(
            flops=4 * nodes * nodes * DH, bytes_accessed=6 * nodes * DH, transcendentals=nodes * nodes
        ),
        name="attend",
    )(place, edges, bias, *queries, *values)


def emit_kernel(place_ref, *refs):
    parts, weights, outs = refs[:4], refs[4:8], refs[8:16]
    held, heads, weight_sem = refs[16:]
    node, head = place_ref[0], place_ref[1]
    far, near = head // 2, head % 2
    copies = []
    for i in range(4):
        copy = pltpu.make_async_copy(weights[i], held.at[node ^ i], weight_sem.at[i])
        copy.start()
        copies.append(copy)
    for i in range(4):
        heads[node ^ i] = parts[i][...]
    attn = jnp.concatenate([heads[i] for i in range(4)], axis=1)
    for copy in copies:
        copy.wait()
    width = outs[0].shape[1]
    for i in (3, 2, 1, 0):
        for side in range(2):
            start = pl.multiple_of((near ^ side) * width, width)
            term = jnp.dot(
                attn, held[far ^ i, :, pl.ds(start, width)], preferred_element_type=jnp.float32
            )
            outs[4 * side + i][...] = term.astype(jnp.bfloat16)


def emit(place, parts, weights):
    rows = parts[0].shape[0]
    depth, cols = weights[0].shape
    flops = 2 * rows * depth * 4 * cols
    moved = 2 * (rows * depth + 4 * depth * cols + 4 * rows * cols)
    return pl.pallas_call(
        emit_kernel,
        out_shape=[jax.ShapeDtypeStruct((rows, cols // 2), jnp.bfloat16)] * 8,
        in_specs=[smem_spec()] + [vmem_spec()] * 4 + [hbm_spec()] * 4,
        out_specs=[vmem_spec()] * 8,
        scratch_shapes=[
            pltpu.VMEM((4, depth, cols), jnp.bfloat16),
            pltpu.VMEM((4, rows, DH), jnp.bfloat16),
            pltpu.SemaphoreType.DMA((4,)),
        ],
        compiler_params=pltpu.CompilerParams(vmem_limit_bytes=20 * 2**20),
        cost_estimate=pl.CostEstimate(flops=flops, bytes_accessed=moved, transcendentals=0),
        name="emit",
    )(place, *parts, *weights)


def exchange_heads(pieces):
    return [pieces[0]] + [swap(pieces[i], "node", i) for i in range(1, 4)]


def one_head_each(node_feats, w_qk, w_val, w_out, edge_types, rel_bias):
    node, head = lax.axis_index("node"), lax.axis_index("head")
    place = jnp.stack([node, head]).astype(jnp.int32)
    edges = lax.all_gather(edge_types, "node", axis=0, tiled=True)
    bias = lax.dynamic_index_in_dim(rel_bias, node, 1, keepdims=False)

    far = {i: swap(node_feats, "head", 2 * i) for i in (3, 2, 1)}
    far[0] = node_feats
    beside = swap(node_feats, "head", 1)
    qk_across, qk_beside = swap(w_qk, "node", 2), swap(w_qk, "node", 1)
    w_val = after(w_val, qk_across, qk_beside, far[1], far[2], far[3], beside, edges)
    val_across, val_beside = swap(w_val, "node", 2), swap(w_val, "node", 1)
    qk_sent = after(qk_across, far[1], far[2], far[3], beside)
    full_qk = [w_qk, qk_beside, qk_across, swap(qk_sent, "node", 1)]
    pieces = [node_feats, beside]
    for i in (1, 2, 3):
        pieces += [far[i], swap(after(far[i], beside), "head", 1)]

    queries = exchange_heads(project(place, pieces, full_qk))
    w_out = after(w_out, val_across, val_beside, *queries)
    out_across, out_beside = swap(w_out, "node", 2), swap(w_out, "node", 1)
    full_val = [w_val, val_beside, val_across, swap(val_across, "node", 1)]
    values = exchange_heads(project(place, pieces, full_val))
    full_out = [w_out, out_beside, out_across, swap(out_across, "node", 1)]
    attn = exchange_heads(attend(place, edges, bias, queries, values))
    terms = emit(place, attn, full_out)
    sums = [None] * 4
    for i in (3, 2, 1, 0):
        near = swap(terms[4 + i], "head", 1)
        sums[i] = terms[i].astype(jnp.float32) + near.astype(jnp.float32)
    total = sums[0]
    for i in (3, 2, 1):
        moved = swap(sums[i].astype(jnp.bfloat16), "head", 2 * i)
        total = total + moved.astype(jnp.float32)
    return total.astype(jnp.bfloat16)


def from_behind(value, axis, by):
    peers = lax.axis_size(axis)
    return lax.ppermute(value, axis, [(i, (i + by) % peers) for i in range(peers)])


def pair_scores(queries, key_rows):
    inv_root = 1.0 / DH**0.5
    return (
        jnp.einsum("qhd,khd->hqk", queries, key_rows, preferred_element_type=jnp.float32) * inv_root
    )


def update(carried, scaled, bias_cols, value_rows, self_mask):
    head_count, query_count, key_count = scaled.shape
    tiles = bias_cols.shape[1]
    biased = (
        scaled.reshape(head_count, tiles, query_count // tiles, key_count)
        + bias_cols[:, :, None, :]
    )
    biased = biased.reshape(head_count, query_count, key_count)
    if self_mask is not None:
        biased = jnp.where(self_mask[None], NEG_BIG, biased)
    top_old, total_old, accum_old = carried
    top_new = jnp.maximum(top_old, jnp.max(biased, axis=2))
    expd = jnp.exp(biased - top_new[:, :, None])
    if self_mask is not None:
        expd = jnp.where(self_mask[None], 0.0, expd)
    factor = jnp.exp(top_old - top_new)
    total_new = total_old * factor + jnp.sum(expd, axis=2)
    product = jnp.einsum(
        "hqk,khd->hqd", expd.astype(jnp.bfloat16), value_rows, preferred_element_type=jnp.float32
    )
    return (top_new, total_new, accum_old * factor[:, :, None] + product)


def on_device(node_feats, w_qk, w_val, w_out, edge_types, rel_bias):
    row_count = node_feats.shape[0]
    col_width = w_qk.shape[1]
    head_count = rel_bias.shape[1]
    tile_rows = edge_types.shape[0]
    full_qk, full_val = (
        lax.all_gather(w_qk, "node", axis=0, tiled=True),
        lax.all_gather(w_val, "node", axis=0, tiled=True),
    )
    shard_piece = lax.all_gather(node_feats, "head", axis=1, tiled=True)
    proj_qk = jnp.dot(shard_piece, full_qk, preferred_element_type=jnp.float32)
    proj_val = jnp.dot(shard_piece, full_val, preferred_element_type=jnp.float32)
    qk_local = proj_qk.astype(jnp.bfloat16)
    val_local = proj_val.astype(jnp.bfloat16)
    queries = qk_local.reshape(row_count, head_count, DH)
    values = val_local.reshape(row_count, head_count, DH)
    relation_ids = jnp.arange(rel_bias.shape[0], dtype=jnp.int32)
    one_hot = (edge_types[:, :, None] == relation_ids[None, None, :]).astype(jnp.float32)
    tile_bias = jnp.einsum("abr,rh->hab", one_hot, rel_bias, precision=lax.Precision.HIGHEST)
    expanded = jnp.repeat(tile_bias, TILE, axis=2)
    my_block = lax.axis_index("node")
    first_row = my_block * row_count
    row_ids = first_row + jnp.arange(row_count, dtype=jnp.int32)
    initial = (
        jnp.full((head_count, row_count), NEG_BIG, jnp.float32),
        jnp.zeros((head_count, row_count), jnp.float32),
        jnp.zeros((head_count, row_count, DH), jnp.float32),
    )
    node_count = lax.axis_size("node")
    rounds = node_count // 2
    own_cols = lax.dynamic_slice_in_dim(expanded, first_row, row_count, 2)
    own_mask = row_ids[:, None] == row_ids[None, :]
    own_state = update(initial, pair_scores(queries, queries), own_cols, values, own_mask)

    def one_round(round_no, carried):
        mine, moving_block, moving_state = carried
        key_flat, value_flat = from_behind((moving_block[0], moving_block[1]), "node", 1)
        bias_moved, top_moved, total_moved, accum_moved = (
            from_behind(moving_state[0].astype(jnp.bfloat16), "node", 1).astype(jnp.float32),
            from_behind(moving_state[1].astype(jnp.bfloat16), "node", 1).astype(jnp.float32),
            from_behind(moving_state[2].astype(jnp.bfloat16), "node", 1).astype(jnp.float32),
            from_behind(moving_state[3].astype(jnp.bfloat16), "node", 1).astype(jnp.float32),
        )
        partner = (my_block - round_no) % node_count
        key_rows = key_flat.reshape(row_count, head_count, DH)
        value_rows = value_flat.reshape(row_count, head_count, DH)
        raw_scores = pair_scores(queries, key_rows)
        mine_cols = lax.dynamic_slice_in_dim(expanded, partner * row_count, row_count, 2)
        mine = update(mine, raw_scores, mine_cols, value_rows, None)
        back_tiles = lax.dynamic_slice_in_dim(bias_moved, my_block * tile_rows, tile_rows, 2)
        back_cols = jnp.repeat(back_tiles, TILE, axis=2)
        passed = update(
            (top_moved, total_moved, accum_moved),
            jnp.transpose(raw_scores, (0, 2, 1)),
            back_cols,
            values,
            None,
        )
        keep_flag = 2 * round_no != node_count
        kept = jax.tree.map(
            lambda fresh, stale: jnp.where(keep_flag, fresh, stale),
            passed,
            (top_moved, total_moved, accum_moved),
        )
        return (mine, (key_flat, value_flat), (bias_moved, kept[0], kept[1], kept[2]))

    start_state = (tile_bias, initial[0], initial[1], initial[2])
    own_state, _, final_moving = lax.fori_loop(
        1, rounds + 1, one_round, (own_state, (qk_local, val_local), start_state)
    )
    top_home, total_home, accum_home = (
        from_behind(final_moving[1].astype(jnp.bfloat16), "node", -rounds).astype(jnp.float32),
        from_behind(final_moving[2].astype(jnp.bfloat16), "node", -rounds).astype(jnp.float32),
        from_behind(final_moving[3].astype(jnp.bfloat16), "node", -rounds).astype(jnp.float32),
    )
    top_fin = jnp.maximum(own_state[0], top_home)
    factor_own = jnp.exp(own_state[0] - top_fin)
    factor_home = jnp.exp(top_home - top_fin)
    total_fin = own_state[1] * factor_own + total_home * factor_home
    accum_fin = own_state[2] * factor_own[:, :, None] + accum_home * factor_home[:, :, None]
    attn_heads = (accum_fin / total_fin[:, :, None]).astype(jnp.bfloat16)
    attn = jnp.transpose(attn_heads, (1, 0, 2)).reshape(row_count, col_width)
    terms = jnp.dot(
        attn, lax.all_gather(w_out, "node", axis=1, tiled=True), preferred_element_type=jnp.float32
    )
    return lax.psum_scatter(terms.astype(jnp.bfloat16), "head", scatter_dimension=1, tiled=True)

def solution(mesh):
    in_specs = (
        P("node", "head"),
        P("node", "head"),
        P("node", "head"),
        P("head", "node"),
        P("node", None),
        P(None, "head"),
    )
    out_specs = P("node", "head")

    def whole(node_feats, w_qk, w_val, w_out, edge_types, rel_bias):
        node_count, head_count = mesh.shape["node"], mesh.shape["head"]
        column_heads = rel_bias.shape[1] // head_count
        fits = (
            node_count == 4
            and head_count == 2 * node_count
            and column_heads == node_count
            and node_feats.shape[0] % (node_count * TILE) == 0
        )
        body = one_head_each if fits else on_device
        mapped = jax.shard_map(
            body, mesh=mesh, in_specs=in_specs, out_specs=out_specs, check_vma=False
        )
        return mapped(node_feats, w_qk, w_val, w_out, edge_types, rel_bias)

    return whole
```

```python
import functools

import jax
import jax.numpy as jnp
from jax import lax
from jax.experimental import pallas as pl
from jax.experimental.pallas import tpu as pltpu
from jax.sharding import PartitionSpec as P

DH = 128
TILE = 128


NEG_BIG = -1e30


def swap(value, axis, mask):
    peers = lax.axis_size(axis)
    return lax.ppermute(value, axis, [(i, i ^ mask) for i in range(peers)])


def after(value, *others):
    return lax.optimization_barrier((value, *others))[0]


def vmem_spec():
    return pl.BlockSpec(memory_space=pltpu.VMEM)


def smem_spec():
    return pl.BlockSpec(memory_space=pltpu.SMEM)


def project_kernel(*refs):
    pieces, weights, outs = refs[:8], refs[8:12], refs[12:16]
    feats, total, heads, piece_sem = refs[16:]
    node, head = lax.axis_index("node"), lax.axis_index("head")
    copies = []
    for i in range(8):
        copy = pltpu.make_async_copy(pieces[i], feats.at[head ^ i], piece_sem.at[i])
        copy.start()
        copies.append(copy)
    for copy in copies:
        copy.wait()
    depth = feats.shape[2]
    for i in range(4):
        for part in range(2):
            term = jnp.dot(
                feats[2 * (node ^ i) + part],
                weights[i][part * depth : (part + 1) * depth, :],
                preferred_element_type=jnp.float32,
            )
            if i == 0 and part == 0:
                total[...] = term
            else:
                total[...] += term
    for i in range(4):
        heads[i] = total[:, i * DH : (i + 1) * DH].astype(jnp.bfloat16)
    for i in range(4):
        outs[i][...] = heads[node ^ i]


def project(pieces, weights):
    rows, depth = pieces[0].shape
    cols = weights[0].shape[1]
    flops = 2 * rows * 8 * depth * cols
    moved = 2 * (8 * rows * depth + 8 * depth * cols + rows * cols)
    return pl.pallas_call(
        project_kernel,
        out_shape=[jax.ShapeDtypeStruct((rows, DH), jnp.bfloat16)] * 4,
        in_specs=[vmem_spec()] * 12,
        out_specs=[vmem_spec()] * 4,
        scratch_shapes=[
            pltpu.VMEM((8, rows, depth), jnp.bfloat16),
            pltpu.VMEM((rows, cols), jnp.float32),
            pltpu.VMEM((4, rows, DH), jnp.bfloat16),
            pltpu.SemaphoreType.DMA((8,)),
        ],
        compiler_params=pltpu.CompilerParams(vmem_limit_bytes=24 * 2**20),
        cost_estimate=pl.CostEstimate(flops=flops, bytes_accessed=moved, transcendentals=0),
        name="project",
    )(*pieces, *weights)


def attend_kernel(bias_ref, *refs):
    edges, queries, values, outs = refs[:4], refs[4:8], refs[8:12], refs[12:16]
    node = lax.axis_index("node")
    inv_root = 1.0 / DH**0.5
    rows = queries[0].shape[0]
    tiles = rows // TILE
    for i in range(4):
        for ti in range(tiles):
            mine = queries[i][ti * TILE : (ti + 1) * TILE, :]
            scores = []
            for j in range(4):
                raw = lax.dot_general(
                    mine, queries[j][...], (((1,), (1,)), ((), ())),
                    preferred_element_type=jnp.float32,
                )
                for tj in range(tiles):
                    relation = edges[i][ti, tiles * (node ^ j) + tj]
                    part = raw[:, tj * TILE : (tj + 1) * TILE] * inv_root + bias_ref[node, relation]
                    if i == j and ti == tj:
                        row_ids = lax.broadcasted_iota(jnp.int32, (TILE, TILE), 0)
                        col_ids = lax.broadcasted_iota(jnp.int32, (TILE, TILE), 1)
                        part = jnp.where(row_ids == col_ids, NEG_BIG, part)
                    scores.append(part)
            top = functools.reduce(jnp.maximum, scores)
            top = jnp.max(top, axis=1, keepdims=True)
            expd = [jnp.exp(part - top) for part in scores]
            total = jnp.sum(functools.reduce(jnp.add, expd), axis=1, keepdims=True)
            mixed = None
            for j in range(4):
                block = jnp.concatenate(
                    [part.astype(jnp.bfloat16) for part in expd[tiles * j : tiles * (j + 1)]], axis=1
                )
                term = jnp.dot(block, values[j][...], preferred_element_type=jnp.float32)
                mixed = term if mixed is None else mixed + term
            outs[i][ti * TILE : (ti + 1) * TILE, :] = (mixed / total).astype(jnp.bfloat16)


def attend(bias, edges, queries, values):
    rows = queries[0].shape[0]
    nodes = 4 * rows
    return pl.pallas_call(
        attend_kernel,
        out_shape=[jax.ShapeDtypeStruct((rows, DH), jnp.bfloat16)] * 4,
        in_specs=[smem_spec()] * 5 + [vmem_spec()] * 8,
        out_specs=[vmem_spec()] * 4,
        compiler_params=pltpu.CompilerParams(vmem_limit_bytes=16 * 2**20),
        cost_estimate=pl.CostEstimate(
            flops=4 * nodes * nodes * DH, bytes_accessed=6 * nodes * DH, transcendentals=nodes * nodes
        ),
        name="attend",
    )(bias, *edges, *queries, *values)


def emit_kernel(*refs):
    parts, weights, outs = refs[:4], refs[4:8], refs[8:16]
    heads, terms = refs[16:]
    node, head = lax.axis_index("node"), lax.axis_index("head")
    far, near = head // 2, head % 2
    for i in range(4):
        heads[node ^ i] = parts[i][...]
    attn = jnp.concatenate([heads[i] for i in range(4)], axis=1)
    width = outs[0].shape[1]
    for i in range(4):
        plane = node ^ i ^ far
        for side in range(2):
            start = pl.multiple_of((near ^ side) * width, width)
            term = jnp.dot(
                attn, weights[i][:, pl.ds(start, width)], preferred_element_type=jnp.float32
            )
            terms[4 * side + plane] = term.astype(jnp.bfloat16)
    for i in range(8):
        outs[i][...] = terms[i]


def emit(parts, weights):
    rows = parts[0].shape[0]
    depth, cols = weights[0].shape
    flops = 2 * rows * depth * 4 * cols
    moved = 2 * (rows * depth + 4 * depth * cols + 4 * rows * cols)
    return pl.pallas_call(
        emit_kernel,
        out_shape=[jax.ShapeDtypeStruct((rows, cols // 2), jnp.bfloat16)] * 8,
        in_specs=[vmem_spec()] * 8,
        out_specs=[vmem_spec()] * 8,
        scratch_shapes=[
            pltpu.VMEM((4, rows, DH), jnp.bfloat16),
            pltpu.VMEM((8, rows, cols // 2), jnp.bfloat16),
        ],
        compiler_params=pltpu.CompilerParams(vmem_limit_bytes=24 * 2**20),
        cost_estimate=pl.CostEstimate(flops=flops, bytes_accessed=moved, transcendentals=0),
        name="emit",
    )(*parts, *weights)


def exchange(pieces):
    return [pieces[0]] + [swap(pieces[i], "node", i) for i in range(1, 4)]


def one_head_each(node_feats, w_qk, w_val, w_out, edge_types, rel_bias):
    edges = exchange([edge_types] * 4)
    far = {i: swap(node_feats, "head", 2 * i) for i in (3, 2, 1)}
    far[0] = node_feats
    near = {0: swap(after(node_feats, *edges), "head", 1)}
    for i in (3, 1, 2):
        near[i] = swap(far[i], "head", 1)
    qk_across, qk_beside = swap(w_qk, "node", 2), swap(w_qk, "node", 1)
    gate = (far[1], far[2], far[3], near[0], near[1], near[3], qk_beside)
    qk_across, *gate = lax.optimization_barrier((qk_across, *gate))
    w_val = after(w_val, qk_across)
    val_across, val_beside = swap(w_val, "node", 2), swap(w_val, "node", 1)
    full_qk = [w_qk, qk_beside, qk_across, swap(qk_across, "node", 1)]
    pieces = [side[i] for i in range(4) for side in (far, near)]

    queries = exchange(project(pieces, full_qk))
    val_across = after(val_across, *queries)
    w_out = after(w_out, val_across, val_beside)
    out_across, out_beside = swap(w_out, "node", 2), swap(w_out, "node", 1)
    full_val = [w_val, val_beside, val_across, swap(val_across, "node", 1)]
    values = exchange(project(pieces, full_val))
    attn = attend(rel_bias.T, edges, queries, values)
    out_across = after(out_across, *attn)
    attn = exchange(attn)
    full_out = [w_out, out_beside, out_across, swap(out_across, "node", 1)]
    terms = emit(attn, full_out)
    other = {3: swap(terms[7], "head", 1), 2: swap(terms[6], "head", 1)}
    other[1] = swap(after(terms[5], other[3]), "head", 1)
    other[0] = swap(after(terms[4], other[2]), "head", 1)
    total = terms[0].astype(jnp.float32) + other[0].astype(jnp.float32)
    for i in (3, 2, 1):
        pair = terms[i].astype(jnp.float32) + other[i].astype(jnp.float32)
        moved = swap(pair.astype(jnp.bfloat16), "head", 2 * i)
        total = total + moved.astype(jnp.float32)
    return total.astype(jnp.bfloat16)


def from_behind(value, axis, by):
    peers = lax.axis_size(axis)
    return lax.ppermute(value, axis, [(i, (i + by) % peers) for i in range(peers)])


def pair_scores(queries, key_rows):
    inv_root = 1.0 / DH**0.5
    return (
        jnp.einsum("qhd,khd->hqk", queries, key_rows, preferred_element_type=jnp.float32) * inv_root
    )


def update(carried, scaled, bias_cols, value_rows, self_mask):
    head_count, query_count, key_count = scaled.shape
    tiles = bias_cols.shape[1]
    biased = (
        scaled.reshape(head_count, tiles, query_count // tiles, key_count)
        + bias_cols[:, :, None, :]
    )
    biased = biased.reshape(head_count, query_count, key_count)
    if self_mask is not None:
        biased = jnp.where(self_mask[None], NEG_BIG, biased)
    top_old, total_old, accum_old = carried
    top_new = jnp.maximum(top_old, jnp.max(biased, axis=2))
    expd = jnp.exp(biased - top_new[:, :, None])
    if self_mask is not None:
        expd = jnp.where(self_mask[None], 0.0, expd)
    factor = jnp.exp(top_old - top_new)
    total_new = total_old * factor + jnp.sum(expd, axis=2)
    product = jnp.einsum(
        "hqk,khd->hqd", expd.astype(jnp.bfloat16), value_rows, preferred_element_type=jnp.float32
    )
    return (top_new, total_new, accum_old * factor[:, :, None] + product)


def on_device(node_feats, w_qk, w_val, w_out, edge_types, rel_bias):
    row_count = node_feats.shape[0]
    col_width = w_qk.shape[1]
    head_count = rel_bias.shape[1]
    tile_rows = edge_types.shape[0]
    full_qk, full_val = (
        lax.all_gather(w_qk, "node", axis=0, tiled=True),
        lax.all_gather(w_val, "node", axis=0, tiled=True),
    )
    shard_piece = lax.all_gather(node_feats, "head", axis=1, tiled=True)
    proj_qk = jnp.dot(shard_piece, full_qk, preferred_element_type=jnp.float32)
    proj_val = jnp.dot(shard_piece, full_val, preferred_element_type=jnp.float32)
    qk_local = proj_qk.astype(jnp.bfloat16)
    val_local = proj_val.astype(jnp.bfloat16)
    queries = qk_local.reshape(row_count, head_count, DH)
    values = val_local.reshape(row_count, head_count, DH)
    relation_ids = jnp.arange(rel_bias.shape[0], dtype=jnp.int32)
    one_hot = (edge_types[:, :, None] == relation_ids[None, None, :]).astype(jnp.float32)
    tile_bias = jnp.einsum("abr,rh->hab", one_hot, rel_bias, precision=lax.Precision.HIGHEST)
    expanded = jnp.repeat(tile_bias, TILE, axis=2)
    my_block = lax.axis_index("node")
    first_row = my_block * row_count
    row_ids = first_row + jnp.arange(row_count, dtype=jnp.int32)
    initial = (
        jnp.full((head_count, row_count), NEG_BIG, jnp.float32),
        jnp.zeros((head_count, row_count), jnp.float32),
        jnp.zeros((head_count, row_count, DH), jnp.float32),
    )
    node_count = lax.axis_size("node")
    rounds = node_count // 2
    own_cols = lax.dynamic_slice_in_dim(expanded, first_row, row_count, 2)
    own_mask = row_ids[:, None] == row_ids[None, :]
    own_state = update(initial, pair_scores(queries, queries), own_cols, values, own_mask)

    def one_round(round_no, carried):
        mine, moving_block, moving_state = carried
        key_flat, value_flat = from_behind((moving_block[0], moving_block[1]), "node", 1)
        bias_moved, top_moved, total_moved, accum_moved = (
            from_behind(moving_state[0].astype(jnp.bfloat16), "node", 1).astype(jnp.float32),
            from_behind(moving_state[1].astype(jnp.bfloat16), "node", 1).astype(jnp.float32),
            from_behind(moving_state[2].astype(jnp.bfloat16), "node", 1).astype(jnp.float32),
            from_behind(moving_state[3].astype(jnp.bfloat16), "node", 1).astype(jnp.float32),
        )
        partner = (my_block - round_no) % node_count
        key_rows = key_flat.reshape(row_count, head_count, DH)
        value_rows = value_flat.reshape(row_count, head_count, DH)
        raw_scores = pair_scores(queries, key_rows)
        mine_cols = lax.dynamic_slice_in_dim(expanded, partner * row_count, row_count, 2)
        mine = update(mine, raw_scores, mine_cols, value_rows, None)
        back_tiles = lax.dynamic_slice_in_dim(bias_moved, my_block * tile_rows, tile_rows, 2)
        back_cols = jnp.repeat(back_tiles, TILE, axis=2)
        passed = update(
            (top_moved, total_moved, accum_moved),
            jnp.transpose(raw_scores, (0, 2, 1)),
            back_cols,
            values,
            None,
        )
        keep_flag = 2 * round_no != node_count
        kept = jax.tree.map(
            lambda fresh, stale: jnp.where(keep_flag, fresh, stale),
            passed,
            (top_moved, total_moved, accum_moved),
        )
        return (mine, (key_flat, value_flat), (bias_moved, kept[0], kept[1], kept[2]))

    start_state = (tile_bias, initial[0], initial[1], initial[2])
    own_state, _, final_moving = lax.fori_loop(
        1, rounds + 1, one_round, (own_state, (qk_local, val_local), start_state)
    )
    top_home, total_home, accum_home = (
        from_behind(final_moving[1].astype(jnp.bfloat16), "node", -rounds).astype(jnp.float32),
        from_behind(final_moving[2].astype(jnp.bfloat16), "node", -rounds).astype(jnp.float32),
        from_behind(final_moving[3].astype(jnp.bfloat16), "node", -rounds).astype(jnp.float32),
    )
    top_fin = jnp.maximum(own_state[0], top_home)
    factor_own = jnp.exp(own_state[0] - top_fin)
    factor_home = jnp.exp(top_home - top_fin)
    total_fin = own_state[1] * factor_own + total_home * factor_home
    accum_fin = own_state[2] * factor_own[:, :, None] + accum_home * factor_home[:, :, None]
    attn_heads = (accum_fin / total_fin[:, :, None]).astype(jnp.bfloat16)
    attn = jnp.transpose(attn_heads, (1, 0, 2)).reshape(row_count, col_width)
    terms = jnp.dot(
        attn, lax.all_gather(w_out, "node", axis=1, tiled=True), preferred_element_type=jnp.float32
    )
    return lax.psum_scatter(terms.astype(jnp.bfloat16), "head", scatter_dimension=1, tiled=True)

def solution(mesh):
    in_specs = (
        P("node", "head"),
        P("node", "head"),
        P("node", "head"),
        P("head", "node"),
        P("node", None),
        P(None, "head"),
    )
    out_specs = P("node", "head")

    def whole(node_feats, w_qk, w_val, w_out, edge_types, rel_bias):
        node_count, head_count = mesh.shape["node"], mesh.shape["head"]
        column_heads = rel_bias.shape[1] // head_count
        fits = (
            node_count == 4
            and head_count == 2 * node_count
            and column_heads == node_count
            and node_feats.shape[0] % (node_count * TILE) == 0
        )
        body = one_head_each if fits else on_device
        mapped = jax.shard_map(
            body, mesh=mesh, in_specs=in_specs, out_specs=out_specs, check_vma=False
        )
        return mapped(node_feats, w_qk, w_val, w_out, edge_types, rel_bias)

    return whole
```

```python
import functools

import jax
import jax.numpy as jnp
from jax import lax
from jax.experimental import pallas as pl
from jax.experimental.pallas import tpu as pltpu
from jax.sharding import PartitionSpec as P

DH = 128
TILE = 128


NEG_BIG = -1e30


def swap(value, axis, mask):
    peers = lax.axis_size(axis)
    return lax.ppermute(value, axis, [(i, i ^ mask) for i in range(peers)])


def after(value, *others):
    return lax.optimization_barrier((value, *others))[0]


def vmem_spec():
    return pl.BlockSpec(memory_space=pltpu.VMEM)


def smem_spec():
    return pl.BlockSpec(memory_space=pltpu.SMEM)


def in_line(node, head):
    return node // 2 == head // 4


def sort_kernel(close_ref, distant_ref, send_ref, keep_ref):
    lined = in_line(lax.axis_index("node"), lax.axis_index("head"))

    @pl.when(lined)
    def _():
        send_ref[...] = distant_ref[...]
        keep_ref[...] = close_ref[...]

    @pl.when(jnp.logical_not(lined))
    def _():
        send_ref[...] = close_ref[...]
        keep_ref[...] = distant_ref[...]


def sort(close, distant):
    shape = jax.ShapeDtypeStruct(close.shape, close.dtype)
    return pl.pallas_call(
        sort_kernel,
        out_shape=[shape, shape],
        in_specs=[vmem_spec()] * 2,
        out_specs=[vmem_spec()] * 2,
        compiler_params=pltpu.CompilerParams(vmem_limit_bytes=8 * 2**20),
        cost_estimate=pl.CostEstimate(flops=0, bytes_accessed=8 * close.size, transcendentals=0),
        name="sort",
    )(close, distant)


def project_kernel(*refs):
    pieces, weights, keep_ref, send_ref = refs[:8], refs[8:10], refs[10], refs[11]
    feats, total, piece_sem = refs[12:]
    node, head = lax.axis_index("node"), lax.axis_index("head")
    side, core = node // 2, node % 2
    slot = (head // 2) % 2 ^ jnp.where(in_line(node, head), 0, 1)
    near = head % 2
    copies = []
    for i in range(8):
        block, plane, other = i // 4, (i // 2) % 2, i % 2
        place = 4 * block + 2 * (slot ^ plane) + (near ^ other)
        copy = pltpu.make_async_copy(pieces[i], feats.at[place], piece_sem.at[i])
        copy.start()
        copies.append(copy)
    for copy in copies:
        copy.wait()
    _, rows, depth = feats.shape
    width = keep_ref.shape[1]
    for block in range(2):
        for i in range(2):
            for part in range(2):
                term = jnp.dot(
                    feats[4 * block + 2 * (core ^ i) + part],
                    weights[i][part * depth : (part + 1) * depth, :],
                    preferred_element_type=jnp.float32,
                )
                if i == 0 and part == 0:
                    total[...] = term
                else:
                    total[...] += term
        mine = pl.ds(pl.multiple_of(side * width, width), width)
        theirs = pl.ds(pl.multiple_of((1 - side) * width, width), width)
        keep_ref[block * rows : (block + 1) * rows, :] = total[:, mine]
        send_ref[block * rows : (block + 1) * rows, :] = total[:, theirs].astype(jnp.bfloat16)


def project(pieces, weights):
    rows, depth = pieces[0].shape
    cols = weights[0].shape[1]
    flops = 2 * 2 * rows * 4 * depth * cols
    moved = 2 * (8 * rows * depth + 4 * depth * cols + 3 * rows * cols)
    return pl.pallas_call(
        project_kernel,
        out_shape=[
            jax.ShapeDtypeStruct((2 * rows, cols // 2), jnp.float32),
            jax.ShapeDtypeStruct((2 * rows, cols // 2), jnp.bfloat16),
        ],
        in_specs=[vmem_spec()] * 10,
        out_specs=[vmem_spec()] * 2,
        scratch_shapes=[
            pltpu.VMEM((8, rows, depth), jnp.bfloat16),
            pltpu.VMEM((rows, cols), jnp.float32),
            pltpu.SemaphoreType.DMA((8,)),
        ],
        compiler_params=pltpu.CompilerParams(vmem_limit_bytes=20 * 2**20),
        cost_estimate=pl.CostEstimate(flops=flops, bytes_accessed=moved, transcendentals=0),
        name="project",
    )(*pieces, *weights)


def combine_kernel(keep_ref, moved_ref, mine_ref, give_ref):
    core = lax.axis_index("node") % 2
    rows = keep_ref.shape[0] // 2
    for out_ref, place in ((mine_ref, core), (give_ref, 1 - core)):
        cols = pl.ds(pl.multiple_of(place * DH, DH), DH)
        for block in range(2):
            here = slice(block * rows, (block + 1) * rows)
            there = slice((1 - block) * rows, (2 - block) * rows)
            both = keep_ref[here, cols] + moved_ref[there, cols].astype(jnp.float32)
            out_ref[here, :] = both.astype(jnp.bfloat16)


def combine(keep, moved):
    shape = jax.ShapeDtypeStruct((keep.shape[0], DH), jnp.bfloat16)
    return pl.pallas_call(
        combine_kernel,
        out_shape=[shape, shape],
        in_specs=[vmem_spec()] * 2,
        out_specs=[vmem_spec()] * 2,
        compiler_params=pltpu.CompilerParams(vmem_limit_bytes=8 * 2**20),
        cost_estimate=pl.CostEstimate(flops=keep.size, bytes_accessed=8 * keep.size, transcendentals=0),
        name="combine",
    )(keep, moved)


def attend_kernel(bias_ref, *refs):
    edges, held, outs = refs[:4], refs[4:8], refs[8:12]
    node = lax.axis_index("node")
    inv_root = 1.0 / DH**0.5
    rows = outs[0].shape[0]
    tiles = rows // TILE

    def block_of(pair, i):
        return pair[i % 2], (i // 2) * rows

    for i in range(4):
        for ti in range(tiles):
            ref, base = block_of(held[:2], i)
            mine = ref[base + ti * TILE : base + (ti + 1) * TILE, :]
            scores = []
            for j in range(4):
                ref, base = block_of(held[:2], j)
                raw = lax.dot_general(
                    mine, ref[base : base + rows, :], (((1,), (1,)), ((), ())),
                    preferred_element_type=jnp.float32,
                )
                for tj in range(tiles):
                    relation = edges[i][ti, tiles * (node ^ j) + tj]
                    part = raw[:, tj * TILE : (tj + 1) * TILE] * inv_root + bias_ref[node, relation]
                    if i == j and ti == tj:
                        row_ids = lax.broadcasted_iota(jnp.int32, (TILE, TILE), 0)
                        col_ids = lax.broadcasted_iota(jnp.int32, (TILE, TILE), 1)
                        part = jnp.where(row_ids == col_ids, NEG_BIG, part)
                    scores.append(part)
            top = functools.reduce(jnp.maximum, scores)
            top = jnp.max(top, axis=1, keepdims=True)
            expd = [jnp.exp(part - top) for part in scores]
            total = jnp.sum(functools.reduce(jnp.add, expd), axis=1, keepdims=True)
            mixed = None
            for j in range(4):
                block = jnp.concatenate(
                    [part.astype(jnp.bfloat16) for part in expd[tiles * j : tiles * (j + 1)]], axis=1
                )
                ref, base = block_of(held[2:], j)
                term = jnp.dot(block, ref[base : base + rows, :], preferred_element_type=jnp.float32)
                mixed = term if mixed is None else mixed + term
            outs[i][ti * TILE : (ti + 1) * TILE, :] = (mixed / total).astype(jnp.bfloat16)


def attend(bias, edges, queries, values):
    rows = queries[0].shape[0] // 2
    nodes = 4 * rows
    return pl.pallas_call(
        attend_kernel,
        out_shape=[jax.ShapeDtypeStruct((rows, DH), jnp.bfloat16)] * 4,
        in_specs=[smem_spec()] * 5 + [vmem_spec()] * 4,
        out_specs=[vmem_spec()] * 4,
        compiler_params=pltpu.CompilerParams(vmem_limit_bytes=16 * 2**20),
        cost_estimate=pl.CostEstimate(
            flops=4 * nodes * nodes * DH, bytes_accessed=6 * nodes * DH, transcendentals=nodes * nodes
        ),
        name="attend",
    )(bias, *edges, *queries, *values)


def emit_kernel(counts, *refs):
    parts, refs = refs[:4], refs[4:]
    weights = []
    for count in counts:
        weights.append(refs[:count])
        refs = refs[count:]
    outs, heads, terms = refs[:8], refs[8], refs[9]
    node, head = lax.axis_index("node"), lax.axis_index("head")
    far, near = head // 2, head % 2
    for i in range(4):
        heads[node ^ i] = parts[i][...]
    attn = jnp.concatenate([heads[i] for i in range(4)], axis=1)
    width = outs[0].shape[1]
    for i in range(4):
        plane = node ^ i ^ far
        for side in range(2):
            start = pl.multiple_of((near ^ side) * width, width)
            total, first = None, 0
            for ref in weights[i]:
                last = first + ref.shape[0]
                term = jnp.dot(
                    attn[:, first:last], ref[:, pl.ds(start, width)],
                    preferred_element_type=jnp.float32,
                )
                total, first = term if total is None else total + term, last
            terms[4 * side + plane] = total.astype(jnp.bfloat16)
    for i in range(8):
        outs[i][...] = terms[i]


def emit(parts, weights):
    rows = parts[0].shape[0]
    depth, cols = weights[0][0].shape
    counts = [len(pieces) for pieces in weights]
    flops = 2 * rows * depth * 4 * cols
    moved = 2 * (rows * depth + 4 * depth * cols + 4 * rows * cols)
    return pl.pallas_call(
        functools.partial(emit_kernel, counts),
        out_shape=[jax.ShapeDtypeStruct((rows, cols // 2), jnp.bfloat16)] * 8,
        in_specs=[vmem_spec()] * (4 + sum(counts)),
        out_specs=[vmem_spec()] * 8,
        scratch_shapes=[
            pltpu.VMEM((4, rows, DH), jnp.bfloat16),
            pltpu.VMEM((8, rows, cols // 2), jnp.bfloat16),
        ],
        compiler_params=pltpu.CompilerParams(vmem_limit_bytes=20 * 2**20),
        cost_estimate=pl.CostEstimate(flops=flops, bytes_accessed=moved, transcendentals=0),
        name="emit",
    )(*parts, *[piece for pieces in weights for piece in pieces])


def one_head_each(node_feats, w_qk, w_val, w_out, edge_types, rel_bias):
    depth = w_out.shape[0]
    across = functools.partial(swap, axis="node", mask=2)
    beside = functools.partial(swap, axis="node", mask=1)
    along = functools.partial(swap, axis="head", mask=1)

    edges = [edge_types] + [swap(edge_types, "node", i) for i in range(1, 4)]
    far = {i: swap(node_feats, "head", 2 * i) for i in (3, 2, 1)}
    out_first = across(after(w_out[: depth // 2], *edges))
    send_0, keep_0 = sort(node_feats, far[3])
    moved_0, keep_0y = across(send_0), along(keep_0)
    out_second = across(after(w_out[depth // 2 : 3 * depth // 4], moved_0, out_first))
    moved_0y = along(moved_0)
    send_1, keep_1 = sort(*lax.optimization_barrier((far[1], far[2], keep_0y))[:2])
    moved_1, keep_1y = across(send_1), along(keep_1)
    moved_1y = along(moved_1)
    out_third = across(after(w_out[3 * depth // 4 :], moved_1, out_second))
    qk_beside, val_beside, out_beside = beside(w_qk), beside(w_val), beside(w_out)
    qk_beside = after(qk_beside, out_first)

    pieces = [keep_0, keep_0y, keep_1, keep_1y, moved_0, moved_0y, moved_1, moved_1y]
    qk_keep, qk_send = project(pieces, [w_qk, qk_beside])
    qk_moved = across(after(qk_send, out_third))
    val_keep, val_send = project(pieces, [w_val, val_beside])
    val_moved = across(after(val_send, out_third))
    qk_mine, qk_give = combine(qk_keep, qk_moved)
    qk_theirs = beside(qk_give)
    val_mine, val_give = combine(val_keep, val_moved)
    val_theirs = beside(val_give)
    attn = attend(rel_bias.T, edges, [qk_mine, qk_theirs], [val_mine, val_theirs])
    attn = [attn[0]] + [swap(attn[i], "node", i) for i in range(1, 4)]

    out_across = [out_first, out_second, out_third]
    out_diagonal = [beside(after(piece, qk_moved)) for piece in out_across]
    terms = emit(attn, [[w_out], [out_beside], out_across, out_diagonal])
    total, other, pairs = None, {}, {}
    for i in (3, 2, 1, 0):
        send = terms[4 + i]
        if i < 2:
            send = after(send, pairs[i + 2])
        other[i] = along(send)
        pair = terms[i].astype(jnp.float32) + other[i].astype(jnp.float32)
        if i > 0:
            pairs[i] = pair.astype(jnp.bfloat16)
        else:
            total = pair
    for i in (3, 2, 1):
        total = total + swap(pairs[i], "head", 2 * i).astype(jnp.float32)
    return total.astype(jnp.bfloat16)


def from_behind(value, axis, by):
    peers = lax.axis_size(axis)
    return lax.ppermute(value, axis, [(i, (i + by) % peers) for i in range(peers)])


def pair_scores(queries, key_rows):
    inv_root = 1.0 / DH**0.5
    return (
        jnp.einsum("qhd,khd->hqk", queries, key_rows, preferred_element_type=jnp.float32) * inv_root
    )


def update(carried, scaled, bias_cols, value_rows, self_mask):
    head_count, query_count, key_count = scaled.shape
    tiles = bias_cols.shape[1]
    biased = (
        scaled.reshape(head_count, tiles, query_count // tiles, key_count)
        + bias_cols[:, :, None, :]
    )
    biased = biased.reshape(head_count, query_count, key_count)
    if self_mask is not None:
        biased = jnp.where(self_mask[None], NEG_BIG, biased)
    top_old, total_old, accum_old = carried
    top_new = jnp.maximum(top_old, jnp.max(biased, axis=2))
    expd = jnp.exp(biased - top_new[:, :, None])
    if self_mask is not None:
        expd = jnp.where(self_mask[None], 0.0, expd)
    factor = jnp.exp(top_old - top_new)
    total_new = total_old * factor + jnp.sum(expd, axis=2)
    product = jnp.einsum(
        "hqk,khd->hqd", expd.astype(jnp.bfloat16), value_rows, preferred_element_type=jnp.float32
    )
    return (top_new, total_new, accum_old * factor[:, :, None] + product)


def on_device(node_feats, w_qk, w_val, w_out, edge_types, rel_bias):
    row_count = node_feats.shape[0]
    col_width = w_qk.shape[1]
    head_count = rel_bias.shape[1]
    tile_rows = edge_types.shape[0]
    full_qk, full_val = (
        lax.all_gather(w_qk, "node", axis=0, tiled=True),
        lax.all_gather(w_val, "node", axis=0, tiled=True),
    )
    shard_piece = lax.all_gather(node_feats, "head", axis=1, tiled=True)
    proj_qk = jnp.dot(shard_piece, full_qk, preferred_element_type=jnp.float32)
    proj_val = jnp.dot(shard_piece, full_val, preferred_element_type=jnp.float32)
    qk_local = proj_qk.astype(jnp.bfloat16)
    val_local = proj_val.astype(jnp.bfloat16)
    queries = qk_local.reshape(row_count, head_count, DH)
    values = val_local.reshape(row_count, head_count, DH)
    relation_ids = jnp.arange(rel_bias.shape[0], dtype=jnp.int32)
    one_hot = (edge_types[:, :, None] == relation_ids[None, None, :]).astype(jnp.float32)
    tile_bias = jnp.einsum("abr,rh->hab", one_hot, rel_bias, precision=lax.Precision.HIGHEST)
    expanded = jnp.repeat(tile_bias, TILE, axis=2)
    my_block = lax.axis_index("node")
    first_row = my_block * row_count
    row_ids = first_row + jnp.arange(row_count, dtype=jnp.int32)
    initial = (
        jnp.full((head_count, row_count), NEG_BIG, jnp.float32),
        jnp.zeros((head_count, row_count), jnp.float32),
        jnp.zeros((head_count, row_count, DH), jnp.float32),
    )
    node_count = lax.axis_size("node")
    rounds = node_count // 2
    own_cols = lax.dynamic_slice_in_dim(expanded, first_row, row_count, 2)
    own_mask = row_ids[:, None] == row_ids[None, :]
    own_state = update(initial, pair_scores(queries, queries), own_cols, values, own_mask)

    def one_round(round_no, carried):
        mine, moving_block, moving_state = carried
        key_flat, value_flat = from_behind((moving_block[0], moving_block[1]), "node", 1)
        bias_moved, top_moved, total_moved, accum_moved = (
            from_behind(moving_state[0].astype(jnp.bfloat16), "node", 1).astype(jnp.float32),
            from_behind(moving_state[1].astype(jnp.bfloat16), "node", 1).astype(jnp.float32),
            from_behind(moving_state[2].astype(jnp.bfloat16), "node", 1).astype(jnp.float32),
            from_behind(moving_state[3].astype(jnp.bfloat16), "node", 1).astype(jnp.float32),
        )
        partner = (my_block - round_no) % node_count
        key_rows = key_flat.reshape(row_count, head_count, DH)
        value_rows = value_flat.reshape(row_count, head_count, DH)
        raw_scores = pair_scores(queries, key_rows)
        mine_cols = lax.dynamic_slice_in_dim(expanded, partner * row_count, row_count, 2)
        mine = update(mine, raw_scores, mine_cols, value_rows, None)
        back_tiles = lax.dynamic_slice_in_dim(bias_moved, my_block * tile_rows, tile_rows, 2)
        back_cols = jnp.repeat(back_tiles, TILE, axis=2)
        passed = update(
            (top_moved, total_moved, accum_moved),
            jnp.transpose(raw_scores, (0, 2, 1)),
            back_cols,
            values,
            None,
        )
        keep_flag = 2 * round_no != node_count
        kept = jax.tree.map(
            lambda fresh, stale: jnp.where(keep_flag, fresh, stale),
            passed,
            (top_moved, total_moved, accum_moved),
        )
        return (mine, (key_flat, value_flat), (bias_moved, kept[0], kept[1], kept[2]))

    start_state = (tile_bias, initial[0], initial[1], initial[2])
    own_state, _, final_moving = lax.fori_loop(
        1, rounds + 1, one_round, (own_state, (qk_local, val_local), start_state)
    )
    top_home, total_home, accum_home = (
        from_behind(final_moving[1].astype(jnp.bfloat16), "node", -rounds).astype(jnp.float32),
        from_behind(final_moving[2].astype(jnp.bfloat16), "node", -rounds).astype(jnp.float32),
        from_behind(final_moving[3].astype(jnp.bfloat16), "node", -rounds).astype(jnp.float32),
    )
    top_fin = jnp.maximum(own_state[0], top_home)
    factor_own = jnp.exp(own_state[0] - top_fin)
    factor_home = jnp.exp(top_home - top_fin)
    total_fin = own_state[1] * factor_own + total_home * factor_home
    accum_fin = own_state[2] * factor_own[:, :, None] + accum_home * factor_home[:, :, None]
    attn_heads = (accum_fin / total_fin[:, :, None]).astype(jnp.bfloat16)
    attn = jnp.transpose(attn_heads, (1, 0, 2)).reshape(row_count, col_width)
    terms = jnp.dot(
        attn, lax.all_gather(w_out, "node", axis=1, tiled=True), preferred_element_type=jnp.float32
    )
    return lax.psum_scatter(terms.astype(jnp.bfloat16), "head", scatter_dimension=1, tiled=True)

def solution(mesh):
    in_specs = (
        P("node", "head"),
        P("node", "head"),
        P("node", "head"),
        P("head", "node"),
        P("node", None),
        P(None, "head"),
    )
    out_specs = P("node", "head")

    def whole(node_feats, w_qk, w_val, w_out, edge_types, rel_bias):
        node_count, head_count = mesh.shape["node"], mesh.shape["head"]
        column_heads = rel_bias.shape[1] // head_count
        fits = (
            node_count == 4
            and head_count == 2 * node_count
            and column_heads == node_count
            and node_feats.shape[0] % (node_count * TILE) == 0
        )
        body = one_head_each if fits else on_device
        mapped = jax.shard_map(
            body, mesh=mesh, in_specs=in_specs, out_specs=out_specs, check_vma=False
        )
        return mapped(node_feats, w_qk, w_val, w_out, edge_types, rel_bias)

    return whole
```

```python
import functools

import jax
import jax.numpy as jnp
from jax import lax
from jax.experimental import pallas as pl
from jax.experimental.pallas import tpu as pltpu
from jax.sharding import PartitionSpec as P

DH = 128
TILE = 128


NEG_BIG = -1e30


def swap(value, axis, mask):
    peers = lax.axis_size(axis)
    return lax.ppermute(value, axis, [(i, i ^ mask) for i in range(peers)])


def after(value, *others):
    return lax.optimization_barrier((value, *others))[0]


def vmem_spec():
    return pl.BlockSpec(memory_space=pltpu.VMEM)


def smem_spec():
    return pl.BlockSpec(memory_space=pltpu.SMEM)


def in_line(node, head):
    return node // 2 == head // 4


def sort_kernel(close_ref, distant_ref, first_ref, second_ref, keep_ref):
    lined = in_line(lax.axis_index("node"), lax.axis_index("head"))
    half = first_ref.shape[0]

    def place(send_ref, held_ref):
        first_ref[...] = send_ref[:half, :]
        second_ref[...] = send_ref[half:, :]
        keep_ref[...] = held_ref[...]

    @pl.when(lined)
    def _():
        place(distant_ref, close_ref)

    @pl.when(jnp.logical_not(lined))
    def _():
        place(close_ref, distant_ref)


def sort(close, distant):
    rows, cols = close.shape
    half = jax.ShapeDtypeStruct((rows // 2, cols), close.dtype)
    return pl.pallas_call(
        sort_kernel,
        out_shape=[half, half, jax.ShapeDtypeStruct((rows, cols), close.dtype)],
        in_specs=[vmem_spec()] * 2,
        out_specs=[vmem_spec()] * 3,
        compiler_params=pltpu.CompilerParams(vmem_limit_bytes=8 * 2**20),
        cost_estimate=pl.CostEstimate(flops=0, bytes_accessed=8 * close.size, transcendentals=0),
        name="sort",
    )(close, distant)


def project_kernel(*refs):
    pieces, weights, keep_ref, send_ref = refs[:12], refs[12:14], refs[14], refs[15]
    feats, total, piece_sem = refs[16:]
    node, head = lax.axis_index("node"), lax.axis_index("head")
    side, core = node // 2, node % 2
    slot = (head // 2) % 2 ^ jnp.where(in_line(node, head), 0, 1)
    near = head % 2
    _, rows, depth = feats.shape
    copies = []
    for i in range(12):
        if i < 4:
            block, plane, other, start, count = 0, i // 2, i % 2, 0, rows
        else:
            block, plane, other = 1, (i - 4) // 4, (i - 4) // 2 % 2
            start, count = i % 2 * (rows // 2), rows // 2
        place = 4 * block + 2 * (slot ^ plane) + (near ^ other)
        copy = pltpu.make_async_copy(
            pieces[i], feats.at[place, pl.ds(start, count)], piece_sem.at[i]
        )
        copy.start()
        copies.append(copy)
    for copy in copies:
        copy.wait()
    width = keep_ref.shape[1]
    for block in range(2):
        for i in range(2):
            for part in range(2):
                term = jnp.dot(
                    feats[4 * block + 2 * (core ^ i) + part],
                    weights[i][part * depth : (part + 1) * depth, :],
                    preferred_element_type=jnp.float32,
                )
                if i == 0 and part == 0:
                    total[...] = term
                else:
                    total[...] += term
        mine = pl.ds(pl.multiple_of(side * width, width), width)
        theirs = pl.ds(pl.multiple_of((1 - side) * width, width), width)
        keep_ref[block * rows : (block + 1) * rows, :] = total[:, mine]
        send_ref[block * rows : (block + 1) * rows, :] = total[:, theirs].astype(jnp.bfloat16)


def project(pieces, weights):
    rows, depth = pieces[0].shape
    cols = weights[0].shape[1]
    flops = 2 * 2 * rows * 4 * depth * cols
    moved = 2 * (8 * rows * depth + 4 * depth * cols + 3 * rows * cols)
    return pl.pallas_call(
        project_kernel,
        out_shape=[
            jax.ShapeDtypeStruct((2 * rows, cols // 2), jnp.float32),
            jax.ShapeDtypeStruct((2 * rows, cols // 2), jnp.bfloat16),
        ],
        in_specs=[vmem_spec()] * 14,
        out_specs=[vmem_spec()] * 2,
        scratch_shapes=[
            pltpu.VMEM((8, rows, depth), jnp.bfloat16),
            pltpu.VMEM((rows, cols), jnp.float32),
            pltpu.SemaphoreType.DMA((12,)),
        ],
        compiler_params=pltpu.CompilerParams(vmem_limit_bytes=20 * 2**20),
        cost_estimate=pl.CostEstimate(flops=flops, bytes_accessed=moved, transcendentals=0),
        name="project",
    )(*pieces, *weights)


def combine_kernel(keep_ref, moved_ref, mine_ref, give_ref):
    core = lax.axis_index("node") % 2
    rows = keep_ref.shape[0] // 2
    for out_ref, place in ((mine_ref, core), (give_ref, 1 - core)):
        cols = pl.ds(pl.multiple_of(place * DH, DH), DH)
        for block in range(2):
            here = slice(block * rows, (block + 1) * rows)
            there = slice((1 - block) * rows, (2 - block) * rows)
            both = keep_ref[here, cols] + moved_ref[there, cols].astype(jnp.float32)
            out_ref[here, :] = both.astype(jnp.bfloat16)


def combine(keep, moved):
    shape = jax.ShapeDtypeStruct((keep.shape[0], DH), jnp.bfloat16)
    return pl.pallas_call(
        combine_kernel,
        out_shape=[shape, shape],
        in_specs=[vmem_spec()] * 2,
        out_specs=[vmem_spec()] * 2,
        compiler_params=pltpu.CompilerParams(vmem_limit_bytes=8 * 2**20),
        cost_estimate=pl.CostEstimate(flops=keep.size, bytes_accessed=8 * keep.size, transcendentals=0),
        name="combine",
    )(keep, moved)


def weigh_kernel(edge_ref, bias_ref, mine_ref, theirs_ref, weight_ref, total_ref):
    node = lax.axis_index("node")
    inv_root = 1.0 / DH**0.5
    rows = mine_ref.shape[0] // 2
    tiles = rows // TILE
    held = (mine_ref, theirs_ref)
    for i in range(4):
        for ti in range(tiles):
            base = i // 2 * rows + ti * TILE
            queries = held[i % 2][base : base + TILE, :]
            scores = []
            for j in range(4):
                keys = held[j % 2][j // 2 * rows : (j // 2 + 1) * rows, :]
                raw = lax.dot_general(
                    queries, keys, (((1,), (1,)), ((), ())), preferred_element_type=jnp.float32
                )
                for tj in range(tiles):
                    relation = edge_ref[i, ti, tiles * (node ^ j) + tj]
                    part = raw[:, tj * TILE : (tj + 1) * TILE] * inv_root + bias_ref[node, relation]
                    if i == j and ti == tj:
                        row_ids = lax.broadcasted_iota(jnp.int32, (TILE, TILE), 0)
                        col_ids = lax.broadcasted_iota(jnp.int32, (TILE, TILE), 1)
                        part = jnp.where(row_ids == col_ids, NEG_BIG, part)
                    scores.append(part)
            top = functools.reduce(jnp.maximum, scores)
            top = jnp.max(top, axis=1, keepdims=True)
            expd = [jnp.exp(part - top) for part in scores]
            here = slice(i * rows + ti * TILE, i * rows + (ti + 1) * TILE)
            total_ref[here, :] = jnp.sum(functools.reduce(jnp.add, expd), axis=1, keepdims=True)
            for k, part in enumerate(expd):
                weight_ref[here, k * TILE : (k + 1) * TILE] = part.astype(jnp.bfloat16)


def weigh(edges, bias, mine, theirs):
    nodes = 2 * mine.shape[0]
    return pl.pallas_call(
        weigh_kernel,
        out_shape=[
            jax.ShapeDtypeStruct((nodes, nodes), jnp.bfloat16),
            jax.ShapeDtypeStruct((nodes, 1), jnp.float32),
        ],
        in_specs=[smem_spec()] * 2 + [vmem_spec()] * 2,
        out_specs=[vmem_spec()] * 2,
        compiler_params=pltpu.CompilerParams(vmem_limit_bytes=16 * 2**20),
        cost_estimate=pl.CostEstimate(
            flops=2 * nodes * nodes * DH, bytes_accessed=2 * nodes * nodes, transcendentals=nodes * nodes
        ),
        name="weigh",
    )(edges, bias, mine, theirs)


def average_kernel(blocks, weight_ref, total_ref, mine_ref, theirs_ref, *outs):
    rows = mine_ref.shape[0] // 2
    held = (mine_ref, theirs_ref)
    for out_ref, i in zip(outs, blocks):
        here = slice(i * rows, (i + 1) * rows)
        mixed = None
        for j in range(4):
            term = jnp.dot(
                weight_ref[here, j * rows : (j + 1) * rows],
                held[j % 2][j // 2 * rows : (j // 2 + 1) * rows, :],
                preferred_element_type=jnp.float32,
            )
            mixed = term if mixed is None else mixed + term
        out_ref[...] = (mixed / total_ref[here, :]).astype(jnp.bfloat16)


def average(blocks, weights, total, mine, theirs):
    rows = mine.shape[0] // 2
    return pl.pallas_call(
        functools.partial(average_kernel, blocks),
        out_shape=[jax.ShapeDtypeStruct((rows, DH), jnp.bfloat16)] * len(blocks),
        in_specs=[vmem_spec()] * 4,
        out_specs=[vmem_spec()] * len(blocks),
        compiler_params=pltpu.CompilerParams(vmem_limit_bytes=16 * 2**20),
        cost_estimate=pl.CostEstimate(
            flops=8 * len(blocks) * rows * rows * DH, bytes_accessed=weights.size, transcendentals=0
        ),
        name="average",
    )(weights, total, mine, theirs)


def emit_kernel(counts, *refs):
    parts, refs = refs[:4], refs[4:]
    weights = []
    for count in counts:
        weights.append(refs[:count])
        refs = refs[count:]
    outs, heads, terms = refs[:9], refs[9], refs[10]
    node, head = lax.axis_index("node"), lax.axis_index("head")
    far, near = head // 2, head % 2
    for i in range(4):
        heads[node ^ i] = parts[i][...]
    attn = jnp.concatenate([heads[i] for i in range(4)], axis=1)
    width = outs[0].shape[1]
    for i in range(4):
        plane = node ^ i ^ far
        for side in range(2):
            start = pl.multiple_of((near ^ side) * width, width)
            total, first = None, 0
            for ref in weights[i]:
                last = first + ref.shape[0]
                term = jnp.dot(
                    attn[:, first:last], ref[:, pl.ds(start, width)],
                    preferred_element_type=jnp.float32,
                )
                total, first = term if total is None else total + term, last
            terms[4 * side + plane] = total.astype(jnp.bfloat16)
    first = outs[7].shape[0]
    for i in range(7):
        outs[i][...] = terms[i]
    outs[7][...] = terms[7, :first, :]
    outs[8][...] = terms[7, first:, :]


def emit(parts, weights):
    rows = parts[0].shape[0]
    depth, cols = weights[0][0].shape
    counts = [len(pieces) for pieces in weights]
    first = 3 * rows // 8
    flops = 2 * rows * depth * 4 * cols
    moved = 2 * (rows * depth + 4 * depth * cols + 4 * rows * cols)
    return pl.pallas_call(
        functools.partial(emit_kernel, counts),
        out_shape=[jax.ShapeDtypeStruct((rows, cols // 2), jnp.bfloat16)] * 7
        + [jax.ShapeDtypeStruct((part, cols // 2), jnp.bfloat16) for part in (first, rows - first)],
        in_specs=[vmem_spec()] * (4 + sum(counts)),
        out_specs=[vmem_spec()] * 9,
        scratch_shapes=[
            pltpu.VMEM((4, rows, DH), jnp.bfloat16),
            pltpu.VMEM((8, rows, cols // 2), jnp.bfloat16),
        ],
        compiler_params=pltpu.CompilerParams(vmem_limit_bytes=20 * 2**20),
        cost_estimate=pl.CostEstimate(flops=flops, bytes_accessed=moved, transcendentals=0),
        name="emit",
    )(*parts, *[piece for pieces in weights for piece in pieces])


def one_head_each(node_feats, w_qk, w_val, w_out, edge_types, rel_bias):
    depth, rows = w_out.shape[0], node_feats.shape[0]
    across = functools.partial(swap, axis="node", mask=2)
    beside = functools.partial(swap, axis="node", mask=1)
    along = functools.partial(swap, axis="head", mask=1)

    far = {i: swap(node_feats, "head", 2 * i) for i in (3, 2, 1)}
    out_first = across(w_out[: 5 * depth // 8])
    tiles = jnp.stack([edge_types, beside(edge_types)])
    *send_0, keep_0 = sort(node_feats, after(far[3], out_first))
    keep_0y = along(keep_0)
    moved_0 = [across(part) for part in send_0]
    moved_0y = [along(part) for part in moved_0]
    gate = (keep_0y, moved_0[1], moved_0y[0], tiles)
    close, distant = lax.optimization_barrier((far[1], far[2], *gate))[:2]
    *send_1, keep_1 = sort(close, distant)
    moved_1 = [across(part) for part in send_1]
    keep_1y = along(keep_1)
    moved_1y = [along(part) for part in moved_1]
    out_second = across(after(w_out[5 * depth // 8 :], moved_1[1]))
    qk_beside, val_beside = beside(w_qk), beside(w_val)
    edges = jnp.concatenate([tiles, across(after(tiles, moved_1[0]))])

    keep_1y = after(keep_1y, edges)
    pieces = [keep_0, keep_0y, keep_1, keep_1y, *moved_0, *moved_0y, *moved_1, *moved_1y]
    qk_keep, qk_send = project(pieces, [w_qk, qk_beside])
    qk_moved = across(qk_send)
    val_keep, val_send = project(pieces, [w_val, val_beside])
    val_moved = across(val_send)
    qk_mine, qk_give = combine(qk_keep, after(qk_moved, val_send, out_second))
    weights, total = weigh(edges, rel_bias.T, qk_mine, beside(qk_give))
    val_mine, val_give = combine(val_keep, after(val_moved, total))
    attn = average((0, 1, 2, 3), weights, total, val_mine, beside(val_give))
    attn = [attn[0]] + [swap(attn[i], "node", i) for i in range(1, 4)]

    out_across = [out_first, out_second]
    out_beside = beside(after(w_out, moved_1[0]))
    out_diagonal = [beside(after(out_first, moved_1[0])), beside(out_second)]
    terms = emit(attn, [[w_out], [out_beside], out_across, out_diagonal])

    def pair(mine, send):
        return mine.astype(jnp.float32) + along(send).astype(jnp.float32)

    first = terms[7].shape[0]
    pair_3 = [
        pair(terms[3][:first], terms[7]).astype(jnp.bfloat16),
        pair(terms[3][first:], terms[8]).astype(jnp.bfloat16),
    ]
    home_3 = [swap(part, "head", 6) for part in pair_3]
    pair_2 = pair(terms[2], after(terms[6], pair_3[0])).astype(jnp.bfloat16)
    pair_1 = pair(terms[1], after(terms[5], pair_3[1])).astype(jnp.bfloat16)
    total = pair(terms[0], after(terms[4], home_3[0]))
    total = total + swap(pair_2, "head", 4).astype(jnp.float32)
    total = total + swap(after(pair_1, home_3[1]), "head", 2).astype(jnp.float32)
    total = total + jnp.concatenate(home_3).astype(jnp.float32)
    return total.astype(jnp.bfloat16)


def from_behind(value, axis, by):
    peers = lax.axis_size(axis)
    return lax.ppermute(value, axis, [(i, (i + by) % peers) for i in range(peers)])


def pair_scores(queries, key_rows):
    inv_root = 1.0 / DH**0.5
    return (
        jnp.einsum("qhd,khd->hqk", queries, key_rows, preferred_element_type=jnp.float32) * inv_root
    )


def update(carried, scaled, bias_cols, value_rows, self_mask):
    head_count, query_count, key_count = scaled.shape
    tiles = bias_cols.shape[1]
    biased = (
        scaled.reshape(head_count, tiles, query_count // tiles, key_count)
        + bias_cols[:, :, None, :]
    )
    biased = biased.reshape(head_count, query_count, key_count)
    if self_mask is not None:
        biased = jnp.where(self_mask[None], NEG_BIG, biased)
    top_old, total_old, accum_old = carried
    top_new = jnp.maximum(top_old, jnp.max(biased, axis=2))
    expd = jnp.exp(biased - top_new[:, :, None])
    if self_mask is not None:
        expd = jnp.where(self_mask[None], 0.0, expd)
    factor = jnp.exp(top_old - top_new)
    total_new = total_old * factor + jnp.sum(expd, axis=2)
    product = jnp.einsum(
        "hqk,khd->hqd", expd.astype(jnp.bfloat16), value_rows, preferred_element_type=jnp.float32
    )
    return (top_new, total_new, accum_old * factor[:, :, None] + product)


def on_device(node_feats, w_qk, w_val, w_out, edge_types, rel_bias):
    row_count = node_feats.shape[0]
    col_width = w_qk.shape[1]
    head_count = rel_bias.shape[1]
    tile_rows = edge_types.shape[0]
    full_qk, full_val = (
        lax.all_gather(w_qk, "node", axis=0, tiled=True),
        lax.all_gather(w_val, "node", axis=0, tiled=True),
    )
    shard_piece = lax.all_gather(node_feats, "head", axis=1, tiled=True)
    proj_qk = jnp.dot(shard_piece, full_qk, preferred_element_type=jnp.float32)
    proj_val = jnp.dot(shard_piece, full_val, preferred_element_type=jnp.float32)
    qk_local = proj_qk.astype(jnp.bfloat16)
    val_local = proj_val.astype(jnp.bfloat16)
    queries = qk_local.reshape(row_count, head_count, DH)
    values = val_local.reshape(row_count, head_count, DH)
    relation_ids = jnp.arange(rel_bias.shape[0], dtype=jnp.int32)
    one_hot = (edge_types[:, :, None] == relation_ids[None, None, :]).astype(jnp.float32)
    tile_bias = jnp.einsum("abr,rh->hab", one_hot, rel_bias, precision=lax.Precision.HIGHEST)
    expanded = jnp.repeat(tile_bias, TILE, axis=2)
    my_block = lax.axis_index("node")
    first_row = my_block * row_count
    row_ids = first_row + jnp.arange(row_count, dtype=jnp.int32)
    initial = (
        jnp.full((head_count, row_count), NEG_BIG, jnp.float32),
        jnp.zeros((head_count, row_count), jnp.float32),
        jnp.zeros((head_count, row_count, DH), jnp.float32),
    )
    node_count = lax.axis_size("node")
    rounds = node_count // 2
    own_cols = lax.dynamic_slice_in_dim(expanded, first_row, row_count, 2)
    own_mask = row_ids[:, None] == row_ids[None, :]
    own_state = update(initial, pair_scores(queries, queries), own_cols, values, own_mask)

    def one_round(round_no, carried):
        mine, moving_block, moving_state = carried
        key_flat, value_flat = from_behind((moving_block[0], moving_block[1]), "node", 1)
        bias_moved, top_moved, total_moved, accum_moved = (
            from_behind(moving_state[0].astype(jnp.bfloat16), "node", 1).astype(jnp.float32),
            from_behind(moving_state[1].astype(jnp.bfloat16), "node", 1).astype(jnp.float32),
            from_behind(moving_state[2].astype(jnp.bfloat16), "node", 1).astype(jnp.float32),
            from_behind(moving_state[3].astype(jnp.bfloat16), "node", 1).astype(jnp.float32),
        )
        partner = (my_block - round_no) % node_count
        key_rows = key_flat.reshape(row_count, head_count, DH)
        value_rows = value_flat.reshape(row_count, head_count, DH)
        raw_scores = pair_scores(queries, key_rows)
        mine_cols = lax.dynamic_slice_in_dim(expanded, partner * row_count, row_count, 2)
        mine = update(mine, raw_scores, mine_cols, value_rows, None)
        back_tiles = lax.dynamic_slice_in_dim(bias_moved, my_block * tile_rows, tile_rows, 2)
        back_cols = jnp.repeat(back_tiles, TILE, axis=2)
        passed = update(
            (top_moved, total_moved, accum_moved),
            jnp.transpose(raw_scores, (0, 2, 1)),
            back_cols,
            values,
            None,
        )
        keep_flag = 2 * round_no != node_count
        kept = jax.tree.map(
            lambda fresh, stale: jnp.where(keep_flag, fresh, stale),
            passed,
            (top_moved, total_moved, accum_moved),
        )
        return (mine, (key_flat, value_flat), (bias_moved, kept[0], kept[1], kept[2]))

    start_state = (tile_bias, initial[0], initial[1], initial[2])
    own_state, _, final_moving = lax.fori_loop(
        1, rounds + 1, one_round, (own_state, (qk_local, val_local), start_state)
    )
    top_home, total_home, accum_home = (
        from_behind(final_moving[1].astype(jnp.bfloat16), "node", -rounds).astype(jnp.float32),
        from_behind(final_moving[2].astype(jnp.bfloat16), "node", -rounds).astype(jnp.float32),
        from_behind(final_moving[3].astype(jnp.bfloat16), "node", -rounds).astype(jnp.float32),
    )
    top_fin = jnp.maximum(own_state[0], top_home)
    factor_own = jnp.exp(own_state[0] - top_fin)
    factor_home = jnp.exp(top_home - top_fin)
    total_fin = own_state[1] * factor_own + total_home * factor_home
    accum_fin = own_state[2] * factor_own[:, :, None] + accum_home * factor_home[:, :, None]
    attn_heads = (accum_fin / total_fin[:, :, None]).astype(jnp.bfloat16)
    attn = jnp.transpose(attn_heads, (1, 0, 2)).reshape(row_count, col_width)
    terms = jnp.dot(
        attn, lax.all_gather(w_out, "node", axis=1, tiled=True), preferred_element_type=jnp.float32
    )
    return lax.psum_scatter(terms.astype(jnp.bfloat16), "head", scatter_dimension=1, tiled=True)

def solution(mesh):
    in_specs = (
        P("node", "head"),
        P("node", "head"),
        P("node", "head"),
        P("head", "node"),
        P("node", None),
        P(None, "head"),
    )
    out_specs = P("node", "head")

    def whole(node_feats, w_qk, w_val, w_out, edge_types, rel_bias):
        node_count, head_count = mesh.shape["node"], mesh.shape["head"]
        column_heads = rel_bias.shape[1] // head_count
        fits = (
            node_count == 4
            and head_count == 2 * node_count
            and column_heads == node_count
            and node_feats.shape[0] % (node_count * TILE) == 0
        )
        body = one_head_each if fits else on_device
        mapped = jax.shard_map(
            body, mesh=mesh, in_specs=in_specs, out_specs=out_specs, check_vma=False
        )
        return mapped(node_feats, w_qk, w_val, w_out, edge_types, rel_bias)

    return whole
```

```python
import functools

import jax
import jax.numpy as jnp
from jax import lax
from jax.experimental import pallas as pl
from jax.experimental.pallas import tpu as pltpu
from jax.sharding import PartitionSpec as P

DH = 128
TILE = 128


NEG_BIG = -1e30


def swap(value, axis, mask):
    peers = lax.axis_size(axis)
    return lax.ppermute(value, axis, [(i, i ^ mask) for i in range(peers)])


def after(value, *others):
    return lax.optimization_barrier((value, *others))[0]


def vmem_spec():
    return pl.BlockSpec(memory_space=pltpu.VMEM)


def smem_spec():
    return pl.BlockSpec(memory_space=pltpu.SMEM)


def in_line(node, head):
    return node // 2 == head // 4


def sort_kernel(keeps, close_ref, distant_ref, *outs):
    lined = in_line(lax.axis_index("node"), lax.axis_index("head"))

    def place(send_ref, keep_ref):
        for ref, parts in ((keep_ref, outs[:keeps]), (send_ref, outs[keeps:])):
            start = 0
            for part in parts:
                part[...] = ref[start : start + part.shape[0], :]
                start += part.shape[0]

    @pl.when(lined)
    def _():
        place(distant_ref, close_ref)

    @pl.when(jnp.logical_not(lined))
    def _():
        place(close_ref, distant_ref)


def sort(close, distant, keeps, sends):
    rows, cols = close.shape
    shapes = [
        jax.ShapeDtypeStruct((rows // parts, cols), close.dtype)
        for parts in (keeps, sends)
        for _ in range(parts)
    ]
    outs = pl.pallas_call(
        functools.partial(sort_kernel, keeps),
        out_shape=shapes,
        in_specs=[vmem_spec()] * 2,
        out_specs=[vmem_spec()] * len(shapes),
        compiler_params=pltpu.CompilerParams(vmem_limit_bytes=8 * 2**20),
        cost_estimate=pl.CostEstimate(flops=0, bytes_accessed=8 * close.size, transcendentals=0),
        name="sort",
    )(close, distant)
    return outs[:keeps], outs[keeps:]


def project_kernel(counts, *refs):
    pieces = []
    for count in counts:
        pieces.append(refs[:count])
        refs = refs[count:]
    weights, (keep_ref, send_ref, total) = refs[:2], refs[2:]
    node, head = lax.axis_index("node"), lax.axis_index("head")
    side, core = node // 2, node % 2
    slot = (head // 2) % 2 ^ jnp.where(in_line(node, head), 0, 1)
    near = head % 2
    rows, depth = sum(ref.shape[0] for ref in pieces[0]), pieces[0][0].shape[1]
    width = keep_ref.shape[1]
    mine = pl.ds(pl.multiple_of(side * width, width), width)
    theirs = pl.ds(pl.multiple_of((1 - side) * width, width), width)

    def piece(block, plane, other):
        held = pieces[4 * block + 2 * plane + other]
        return jnp.concatenate([ref[...] for ref in held], axis=0)

    def work(flip):
        for block in range(2):
            out = slice(block * rows, (block + 1) * rows)
            sum_so_far = None
            for plane in range(2):
                for other in range(2):
                    start = pl.multiple_of((near ^ other) * depth, depth)
                    term = jnp.dot(
                        piece(block, plane, other),
                        weights[plane ^ flip][pl.ds(start, depth), :],
                        preferred_element_type=jnp.float32,
                    )
                    sum_so_far = term if sum_so_far is None else sum_so_far + term
            total[...] = sum_so_far
            keep_ref[out, :] = total[:, mine]
            send_ref[out, :] = total[:, theirs].astype(jnp.bfloat16)

    for flip in range(2):
        pl.when(slot ^ core == flip)(functools.partial(work, flip))


def project(pieces, weights):
    rows, depth = sum(ref.shape[0] for ref in pieces[0]), pieces[0][0].shape[1]
    cols = weights[0].shape[1]
    counts = [len(held) for held in pieces]
    flops = 2 * 2 * rows * 4 * depth * cols
    moved = 2 * (8 * rows * depth + 4 * depth * cols + 3 * rows * cols)
    return pl.pallas_call(
        functools.partial(project_kernel, counts),
        out_shape=[
            jax.ShapeDtypeStruct((2 * rows, cols // 2), jnp.float32),
            jax.ShapeDtypeStruct((2 * rows, cols // 2), jnp.bfloat16),
        ],
        in_specs=[vmem_spec()] * (sum(counts) + 2),
        out_specs=[vmem_spec()] * 2,
        scratch_shapes=[pltpu.VMEM((rows, cols), jnp.float32)],
        compiler_params=pltpu.CompilerParams(vmem_limit_bytes=20 * 2**20),
        cost_estimate=pl.CostEstimate(flops=flops, bytes_accessed=moved, transcendentals=0),
        name="project",
    )(*[piece for held in pieces for piece in held], *weights)


def combine_kernel(keep_ref, moved_ref, mine_ref, give_ref):
    core = lax.axis_index("node") % 2
    rows = keep_ref.shape[0] // 2
    for out_ref, place in ((mine_ref, core), (give_ref, 1 - core)):
        cols = pl.ds(pl.multiple_of(place * DH, DH), DH)
        for block in range(2):
            here = slice(block * rows, (block + 1) * rows)
            there = slice((1 - block) * rows, (2 - block) * rows)
            both = keep_ref[here, cols] + moved_ref[there, cols].astype(jnp.float32)
            out_ref[here, :] = both.astype(jnp.bfloat16)


def combine(keep, moved):
    shape = jax.ShapeDtypeStruct((keep.shape[0], DH), jnp.bfloat16)
    return pl.pallas_call(
        combine_kernel,
        out_shape=[shape, shape],
        in_specs=[vmem_spec()] * 2,
        out_specs=[vmem_spec()] * 2,
        compiler_params=pltpu.CompilerParams(vmem_limit_bytes=8 * 2**20),
        cost_estimate=pl.CostEstimate(flops=keep.size, bytes_accessed=8 * keep.size, transcendentals=0),
        name="combine",
    )(keep, moved)


def weigh_kernel(edge_ref, bias_ref, mine_ref, theirs_ref, weight_ref, total_ref):
    node = lax.axis_index("node")
    inv_root = 1.0 / DH**0.5
    rows = mine_ref.shape[0] // 2
    tiles = rows // TILE
    held = (mine_ref, theirs_ref)
    for i in range(4):
        for ti in range(tiles):
            base = i // 2 * rows + ti * TILE
            queries = held[i % 2][base : base + TILE, :]
            scores = []
            for j in range(4):
                keys = held[j % 2][j // 2 * rows : (j // 2 + 1) * rows, :]
                raw = lax.dot_general(
                    queries, keys, (((1,), (1,)), ((), ())), preferred_element_type=jnp.float32
                )
                for tj in range(tiles):
                    relation = edge_ref[i, ti, tiles * (node ^ j) + tj]
                    part = raw[:, tj * TILE : (tj + 1) * TILE] * inv_root + bias_ref[node, relation]
                    if i == j and ti == tj:
                        row_ids = lax.broadcasted_iota(jnp.int32, (TILE, TILE), 0)
                        col_ids = lax.broadcasted_iota(jnp.int32, (TILE, TILE), 1)
                        part = jnp.where(row_ids == col_ids, NEG_BIG, part)
                    scores.append(part)
            top = functools.reduce(jnp.maximum, scores)
            top = jnp.max(top, axis=1, keepdims=True)
            expd = [jnp.exp(part - top) for part in scores]
            here = slice(i * rows + ti * TILE, i * rows + (ti + 1) * TILE)
            total_ref[here, :] = jnp.sum(functools.reduce(jnp.add, expd), axis=1, keepdims=True)
            for k, part in enumerate(expd):
                weight_ref[here, k * TILE : (k + 1) * TILE] = part.astype(jnp.bfloat16)


def weigh(edges, bias, mine, theirs):
    nodes = 2 * mine.shape[0]
    return pl.pallas_call(
        weigh_kernel,
        out_shape=[
            jax.ShapeDtypeStruct((nodes, nodes), jnp.bfloat16),
            jax.ShapeDtypeStruct((nodes, 1), jnp.float32),
        ],
        in_specs=[smem_spec()] * 2 + [vmem_spec()] * 2,
        out_specs=[vmem_spec()] * 2,
        compiler_params=pltpu.CompilerParams(vmem_limit_bytes=16 * 2**20),
        cost_estimate=pl.CostEstimate(
            flops=2 * nodes * nodes * DH, bytes_accessed=2 * nodes * nodes, transcendentals=nodes * nodes
        ),
        name="weigh",
    )(edges, bias, mine, theirs)


def average_kernel(blocks, weight_ref, total_ref, mine_ref, theirs_ref, *outs):
    rows = mine_ref.shape[0] // 2
    held = (mine_ref, theirs_ref)
    for out_ref, i in zip(outs, blocks):
        here = slice(i * rows, (i + 1) * rows)
        mixed = None
        for j in range(4):
            term = jnp.dot(
                weight_ref[here, j * rows : (j + 1) * rows],
                held[j % 2][j // 2 * rows : (j // 2 + 1) * rows, :],
                preferred_element_type=jnp.float32,
            )
            mixed = term if mixed is None else mixed + term
        out_ref[...] = (mixed / total_ref[here, :]).astype(jnp.bfloat16)


def average(blocks, weights, total, mine, theirs):
    rows = mine.shape[0] // 2
    return pl.pallas_call(
        functools.partial(average_kernel, blocks),
        out_shape=[jax.ShapeDtypeStruct((rows, DH), jnp.bfloat16)] * len(blocks),
        in_specs=[vmem_spec()] * 4,
        out_specs=[vmem_spec()] * len(blocks),
        compiler_params=pltpu.CompilerParams(vmem_limit_bytes=16 * 2**20),
        cost_estimate=pl.CostEstimate(
            flops=8 * len(blocks) * rows * rows * DH, bytes_accessed=weights.size, transcendentals=0
        ),
        name="average",
    )(weights, total, mine, theirs)


def emit_kernel(counts, *refs):
    parts, refs = refs[:4], refs[4:]
    weights = []
    for count in counts:
        weights.append(refs[:count])
        refs = refs[count:]
    outs, heads, terms = refs[:9], refs[9], refs[10]
    node, head = lax.axis_index("node"), lax.axis_index("head")
    far, near = head // 2, head % 2
    for i in range(4):
        heads[node ^ i] = parts[i][...]
    attn = jnp.concatenate([heads[i] for i in range(4)], axis=1)
    width = outs[0].shape[1]
    for i in range(4):
        plane = node ^ i ^ far
        for side in range(2):
            start = pl.multiple_of((near ^ side) * width, width)
            total, first = None, 0
            for ref in weights[i]:
                last = first + ref.shape[0]
                term = jnp.dot(
                    attn[:, first:last], ref[:, pl.ds(start, width)],
                    preferred_element_type=jnp.float32,
                )
                total, first = term if total is None else total + term, last
            terms[4 * side + plane] = total.astype(jnp.bfloat16)
    first = outs[7].shape[0]
    for i in range(7):
        outs[i][...] = terms[i]
    outs[7][...] = terms[7, :first, :]
    outs[8][...] = terms[7, first:, :]


def emit(parts, weights):
    rows = parts[0].shape[0]
    depth, cols = weights[0][0].shape
    counts = [len(pieces) for pieces in weights]
    first = 3 * rows // 8
    flops = 2 * rows * depth * 4 * cols
    moved = 2 * (rows * depth + 4 * depth * cols + 4 * rows * cols)
    return pl.pallas_call(
        functools.partial(emit_kernel, counts),
        out_shape=[jax.ShapeDtypeStruct((rows, cols // 2), jnp.bfloat16)] * 7
        + [jax.ShapeDtypeStruct((part, cols // 2), jnp.bfloat16) for part in (first, rows - first)],
        in_specs=[vmem_spec()] * (4 + sum(counts)),
        out_specs=[vmem_spec()] * 9,
        scratch_shapes=[
            pltpu.VMEM((4, rows, DH), jnp.bfloat16),
            pltpu.VMEM((8, rows, cols // 2), jnp.bfloat16),
        ],
        compiler_params=pltpu.CompilerParams(vmem_limit_bytes=20 * 2**20),
        cost_estimate=pl.CostEstimate(flops=flops, bytes_accessed=moved, transcendentals=0),
        name="emit",
    )(*parts, *[piece for pieces in weights for piece in pieces])


def one_head_each(node_feats, w_qk, w_val, w_out, edge_types, rel_bias):
    depth, rows = w_out.shape[0], node_feats.shape[0]
    across = functools.partial(swap, axis="node", mask=2)
    beside = functools.partial(swap, axis="node", mask=1)
    along = functools.partial(swap, axis="head", mask=1)

    edges = [edge_types] + [swap(edge_types, "node", i) for i in range(1, 4)]
    far = {i: swap(node_feats, "head", 2 * i) for i in (3, 2, 1)}
    out_first = across(after(w_out[: depth // 2], *edges))
    edges = jnp.stack(edges)
    keep_0, send_0 = sort(node_feats, far[3], 1, 1)
    moved_0, keep_0y = [across(send_0[0])], [along(keep_0[0])]
    out_second = across(after(w_out[depth // 2 : 3 * depth // 4], moved_0[0], out_first))
    moved_0y = [along(moved_0[0])]
    close, distant = lax.optimization_barrier((far[1], far[2], keep_0y[0]))[:2]
    keep_1, send_1 = sort(close, distant, 1, 1)
    moved_1 = [across(part) for part in send_1]
    keep_1y = [along(keep_1[0])]
    moved_1y = [along(part) for part in moved_1]
    out_third = across(after(w_out[3 * depth // 4 :], moved_1[-1], out_second))
    qk_beside, val_beside = beside(w_qk), beside(w_val)
    qk_beside = after(qk_beside, out_first)
    pieces = [keep_0, keep_0y, keep_1, keep_1y, moved_0, moved_0y, moved_1, moved_1y]

    qk_keep, qk_send = project(pieces, [w_qk, qk_beside])
    qk_moved = across(qk_send)
    val_keep, val_send = project(pieces, [w_val, val_beside])
    val_moved = across(val_send)
    qk_mine, qk_give = combine(qk_keep, after(qk_moved, val_send, out_third))
    weights, total = weigh(edges, rel_bias.T, qk_mine, beside(qk_give))
    val_mine, val_give = combine(val_keep, after(val_moved, total))
    attn = average((0, 1, 2, 3), weights, total, val_mine, beside(val_give))
    attn = [attn[0]] + [swap(attn[i], "node", i) for i in range(1, 4)]

    out_across = [out_first, out_second, out_third]
    out_beside = beside(after(w_out, moved_1[0]))
    out_diagonal = [beside(after(piece, moved_1[0])) for piece in out_across[:2]] + [beside(out_third)]
    terms = emit(attn, [[w_out], [out_beside], out_across, out_diagonal])

    def pair(mine, send):
        return mine.astype(jnp.float32) + along(send).astype(jnp.float32)

    first = terms[7].shape[0]
    pair_3 = [
        pair(terms[3][:first], terms[7]).astype(jnp.bfloat16),
        pair(terms[3][first:], terms[8]).astype(jnp.bfloat16),
    ]
    home_3 = [swap(part, "head", 6) for part in pair_3]
    pair_2 = pair(terms[2], after(terms[6], pair_3[0])).astype(jnp.bfloat16)
    pair_1 = pair(terms[1], after(terms[5], pair_3[1])).astype(jnp.bfloat16)
    total = pair(terms[0], after(terms[4], home_3[0]))
    total = total + swap(pair_2, "head", 4).astype(jnp.float32)
    total = total + swap(after(pair_1, home_3[1]), "head", 2).astype(jnp.float32)
    total = total + jnp.concatenate(home_3).astype(jnp.float32)
    return total.astype(jnp.bfloat16)


def from_behind(value, axis, by):
    peers = lax.axis_size(axis)
    return lax.ppermute(value, axis, [(i, (i + by) % peers) for i in range(peers)])


def pair_scores(queries, key_rows):
    inv_root = 1.0 / DH**0.5
    return (
        jnp.einsum("qhd,khd->hqk", queries, key_rows, preferred_element_type=jnp.float32) * inv_root
    )


def update(carried, scaled, bias_cols, value_rows, self_mask):
    head_count, query_count, key_count = scaled.shape
    tiles = bias_cols.shape[1]
    biased = (
        scaled.reshape(head_count, tiles, query_count // tiles, key_count)
        + bias_cols[:, :, None, :]
    )
    biased = biased.reshape(head_count, query_count, key_count)
    if self_mask is not None:
        biased = jnp.where(self_mask[None], NEG_BIG, biased)
    top_old, total_old, accum_old = carried
    top_new = jnp.maximum(top_old, jnp.max(biased, axis=2))
    expd = jnp.exp(biased - top_new[:, :, None])
    if self_mask is not None:
        expd = jnp.where(self_mask[None], 0.0, expd)
    factor = jnp.exp(top_old - top_new)
    total_new = total_old * factor + jnp.sum(expd, axis=2)
    product = jnp.einsum(
        "hqk,khd->hqd", expd.astype(jnp.bfloat16), value_rows, preferred_element_type=jnp.float32
    )
    return (top_new, total_new, accum_old * factor[:, :, None] + product)


def on_device(node_feats, w_qk, w_val, w_out, edge_types, rel_bias):
    row_count = node_feats.shape[0]
    col_width = w_qk.shape[1]
    head_count = rel_bias.shape[1]
    tile_rows = edge_types.shape[0]
    full_qk, full_val = (
        lax.all_gather(w_qk, "node", axis=0, tiled=True),
        lax.all_gather(w_val, "node", axis=0, tiled=True),
    )
    shard_piece = lax.all_gather(node_feats, "head", axis=1, tiled=True)
    proj_qk = jnp.dot(shard_piece, full_qk, preferred_element_type=jnp.float32)
    proj_val = jnp.dot(shard_piece, full_val, preferred_element_type=jnp.float32)
    qk_local = proj_qk.astype(jnp.bfloat16)
    val_local = proj_val.astype(jnp.bfloat16)
    queries = qk_local.reshape(row_count, head_count, DH)
    values = val_local.reshape(row_count, head_count, DH)
    relation_ids = jnp.arange(rel_bias.shape[0], dtype=jnp.int32)
    one_hot = (edge_types[:, :, None] == relation_ids[None, None, :]).astype(jnp.float32)
    tile_bias = jnp.einsum("abr,rh->hab", one_hot, rel_bias, precision=lax.Precision.HIGHEST)
    expanded = jnp.repeat(tile_bias, TILE, axis=2)
    my_block = lax.axis_index("node")
    first_row = my_block * row_count
    row_ids = first_row + jnp.arange(row_count, dtype=jnp.int32)
    initial = (
        jnp.full((head_count, row_count), NEG_BIG, jnp.float32),
        jnp.zeros((head_count, row_count), jnp.float32),
        jnp.zeros((head_count, row_count, DH), jnp.float32),
    )
    node_count = lax.axis_size("node")
    rounds = node_count // 2
    own_cols = lax.dynamic_slice_in_dim(expanded, first_row, row_count, 2)
    own_mask = row_ids[:, None] == row_ids[None, :]
    own_state = update(initial, pair_scores(queries, queries), own_cols, values, own_mask)

    def one_round(round_no, carried):
        mine, moving_block, moving_state = carried
        key_flat, value_flat = from_behind((moving_block[0], moving_block[1]), "node", 1)
        bias_moved, top_moved, total_moved, accum_moved = (
            from_behind(moving_state[0].astype(jnp.bfloat16), "node", 1).astype(jnp.float32),
            from_behind(moving_state[1].astype(jnp.bfloat16), "node", 1).astype(jnp.float32),
            from_behind(moving_state[2].astype(jnp.bfloat16), "node", 1).astype(jnp.float32),
            from_behind(moving_state[3].astype(jnp.bfloat16), "node", 1).astype(jnp.float32),
        )
        partner = (my_block - round_no) % node_count
        key_rows = key_flat.reshape(row_count, head_count, DH)
        value_rows = value_flat.reshape(row_count, head_count, DH)
        raw_scores = pair_scores(queries, key_rows)
        mine_cols = lax.dynamic_slice_in_dim(expanded, partner * row_count, row_count, 2)
        mine = update(mine, raw_scores, mine_cols, value_rows, None)
        back_tiles = lax.dynamic_slice_in_dim(bias_moved, my_block * tile_rows, tile_rows, 2)
        back_cols = jnp.repeat(back_tiles, TILE, axis=2)
        passed = update(
            (top_moved, total_moved, accum_moved),
            jnp.transpose(raw_scores, (0, 2, 1)),
            back_cols,
            values,
            None,
        )
        keep_flag = 2 * round_no != node_count
        kept = jax.tree.map(
            lambda fresh, stale: jnp.where(keep_flag, fresh, stale),
            passed,
            (top_moved, total_moved, accum_moved),
        )
        return (mine, (key_flat, value_flat), (bias_moved, kept[0], kept[1], kept[2]))

    start_state = (tile_bias, initial[0], initial[1], initial[2])
    own_state, _, final_moving = lax.fori_loop(
        1, rounds + 1, one_round, (own_state, (qk_local, val_local), start_state)
    )
    top_home, total_home, accum_home = (
        from_behind(final_moving[1].astype(jnp.bfloat16), "node", -rounds).astype(jnp.float32),
        from_behind(final_moving[2].astype(jnp.bfloat16), "node", -rounds).astype(jnp.float32),
        from_behind(final_moving[3].astype(jnp.bfloat16), "node", -rounds).astype(jnp.float32),
    )
    top_fin = jnp.maximum(own_state[0], top_home)
    factor_own = jnp.exp(own_state[0] - top_fin)
    factor_home = jnp.exp(top_home - top_fin)
    total_fin = own_state[1] * factor_own + total_home * factor_home
    accum_fin = own_state[2] * factor_own[:, :, None] + accum_home * factor_home[:, :, None]
    attn_heads = (accum_fin / total_fin[:, :, None]).astype(jnp.bfloat16)
    attn = jnp.transpose(attn_heads, (1, 0, 2)).reshape(row_count, col_width)
    terms = jnp.dot(
        attn, lax.all_gather(w_out, "node", axis=1, tiled=True), preferred_element_type=jnp.float32
    )
    return lax.psum_scatter(terms.astype(jnp.bfloat16), "head", scatter_dimension=1, tiled=True)

def solution(mesh):
    in_specs = (
        P("node", "head"),
        P("node", "head"),
        P("node", "head"),
        P("head", "node"),
        P("node", None),
        P(None, "head"),
    )
    out_specs = P("node", "head")

    def whole(node_feats, w_qk, w_val, w_out, edge_types, rel_bias):
        node_count, head_count = mesh.shape["node"], mesh.shape["head"]
        column_heads = rel_bias.shape[1] // head_count
        fits = (
            node_count == 4
            and head_count == 2 * node_count
            and column_heads == node_count
            and node_feats.shape[0] % (node_count * TILE) == 0
        )
        body = one_head_each if fits else on_device
        mapped = jax.shard_map(
            body, mesh=mesh, in_specs=in_specs, out_specs=out_specs, check_vma=False
        )
        return mapped(node_feats, w_qk, w_val, w_out, edge_types, rel_bias)

    return whole
```

```python
import functools

import jax
import jax.numpy as jnp
from jax import lax
from jax.experimental import pallas as pl
from jax.experimental.pallas import tpu as pltpu
from jax.sharding import PartitionSpec as P

DH = 128
TILE = 128


NEG_BIG = -1e30


def swap(value, axis, mask):
    peers = lax.axis_size(axis)
    return lax.ppermute(value, axis, [(i, i ^ mask) for i in range(peers)])


def after(value, *others):
    return lax.optimization_barrier((value, *others))[0]


def vmem_spec():
    return pl.BlockSpec(memory_space=pltpu.VMEM)


def smem_spec():
    return pl.BlockSpec(memory_space=pltpu.SMEM)


def in_line(node, head):
    return node // 2 == head // 4


def sort_kernel(keeps, close_ref, distant_ref, *outs):
    lined = in_line(lax.axis_index("node"), lax.axis_index("head"))

    def place(send_ref, keep_ref):
        for ref, parts in ((keep_ref, outs[:keeps]), (send_ref, outs[keeps:])):
            start = 0
            for part in parts:
                part[...] = ref[start : start + part.shape[0], :]
                start += part.shape[0]

    @pl.when(lined)
    def _():
        place(distant_ref, close_ref)

    @pl.when(jnp.logical_not(lined))
    def _():
        place(close_ref, distant_ref)


def sort(close, distant, keeps, sends):
    rows, cols = close.shape
    shapes = [
        jax.ShapeDtypeStruct((rows // parts, cols), close.dtype)
        for parts in (keeps, sends)
        for _ in range(parts)
    ]
    outs = pl.pallas_call(
        functools.partial(sort_kernel, keeps),
        out_shape=shapes,
        in_specs=[vmem_spec()] * 2,
        out_specs=[vmem_spec()] * len(shapes),
        compiler_params=pltpu.CompilerParams(vmem_limit_bytes=8 * 2**20),
        cost_estimate=pl.CostEstimate(flops=0, bytes_accessed=8 * close.size, transcendentals=0),
        name="sort",
    )(close, distant)
    return outs[:keeps], outs[keeps:]


def project_kernel(counts, *refs):
    pieces = []
    for count in counts:
        pieces.append(refs[:count])
        refs = refs[count:]
    weights, (keep_ref, send_ref, total) = refs[:2], refs[2:]
    node, head = lax.axis_index("node"), lax.axis_index("head")
    side, core = node // 2, node % 2
    slot = (head // 2) % 2 ^ jnp.where(in_line(node, head), 0, 1)
    near = head % 2
    rows, depth = sum(ref.shape[0] for ref in pieces[0]), pieces[0][0].shape[1]
    width = keep_ref.shape[1]
    mine = pl.ds(pl.multiple_of(side * width, width), width)
    theirs = pl.ds(pl.multiple_of((1 - side) * width, width), width)

    def piece(block, plane, other):
        held = pieces[4 * block + 2 * plane + other]
        return jnp.concatenate([ref[...] for ref in held], axis=0)

    def work(flip):
        for block in range(2):
            out = slice(block * rows, (block + 1) * rows)
            sum_so_far = None
            for plane in range(2):
                for other in range(2):
                    start = pl.multiple_of((near ^ other) * depth, depth)
                    term = jnp.dot(
                        piece(block, plane, other),
                        weights[plane ^ flip][pl.ds(start, depth), :],
                        preferred_element_type=jnp.float32,
                    )
                    sum_so_far = term if sum_so_far is None else sum_so_far + term
            total[...] = sum_so_far
            keep_ref[out, :] = total[:, mine]
            send_ref[out, :] = total[:, theirs].astype(jnp.bfloat16)

    for flip in range(2):
        pl.when(slot ^ core == flip)(functools.partial(work, flip))


def project(pieces, weights):
    rows, depth = sum(ref.shape[0] for ref in pieces[0]), pieces[0][0].shape[1]
    cols = weights[0].shape[1]
    counts = [len(held) for held in pieces]
    flops = 2 * 2 * rows * 4 * depth * cols
    moved = 2 * (8 * rows * depth + 4 * depth * cols + 3 * rows * cols)
    return pl.pallas_call(
        functools.partial(project_kernel, counts),
        out_shape=[
            jax.ShapeDtypeStruct((2 * rows, cols // 2), jnp.float32),
            jax.ShapeDtypeStruct((2 * rows, cols // 2), jnp.bfloat16),
        ],
        in_specs=[vmem_spec()] * (sum(counts) + 2),
        out_specs=[vmem_spec()] * 2,
        scratch_shapes=[pltpu.VMEM((rows, cols), jnp.float32)],
        compiler_params=pltpu.CompilerParams(vmem_limit_bytes=20 * 2**20),
        cost_estimate=pl.CostEstimate(flops=flops, bytes_accessed=moved, transcendentals=0),
        name="project",
    )(*[piece for held in pieces for piece in held], *weights)


def combine_kernel(keep_ref, moved_ref, mine_ref, give_ref):
    core = lax.axis_index("node") % 2
    rows = keep_ref.shape[0] // 2
    for out_ref, place in ((mine_ref, core), (give_ref, 1 - core)):
        cols = pl.ds(pl.multiple_of(place * DH, DH), DH)
        for block in range(2):
            here = slice(block * rows, (block + 1) * rows)
            there = slice((1 - block) * rows, (2 - block) * rows)
            both = keep_ref[here, cols] + moved_ref[there, cols].astype(jnp.float32)
            out_ref[here, :] = both.astype(jnp.bfloat16)


def combine(keep, moved):
    shape = jax.ShapeDtypeStruct((keep.shape[0], DH), jnp.bfloat16)
    return pl.pallas_call(
        combine_kernel,
        out_shape=[shape, shape],
        in_specs=[vmem_spec()] * 2,
        out_specs=[vmem_spec()] * 2,
        compiler_params=pltpu.CompilerParams(vmem_limit_bytes=8 * 2**20),
        cost_estimate=pl.CostEstimate(flops=keep.size, bytes_accessed=8 * keep.size, transcendentals=0),
        name="combine",
    )(keep, moved)


def weigh_kernel(edge_ref, bias_ref, mine_ref, theirs_ref, weight_ref, total_ref):
    node = lax.axis_index("node")
    inv_root = 1.0 / DH**0.5
    rows = mine_ref.shape[0] // 2
    tiles = rows // TILE
    held = (mine_ref, theirs_ref)
    for i in range(4):
        for ti in range(tiles):
            base = i // 2 * rows + ti * TILE
            queries = held[i % 2][base : base + TILE, :]
            scores = []
            for j in range(4):
                keys = held[j % 2][j // 2 * rows : (j // 2 + 1) * rows, :]
                raw = lax.dot_general(
                    queries, keys, (((1,), (1,)), ((), ())), preferred_element_type=jnp.float32
                )
                for tj in range(tiles):
                    relation = edge_ref[i, ti, tiles * (node ^ j) + tj]
                    part = raw[:, tj * TILE : (tj + 1) * TILE] * inv_root + bias_ref[node, relation]
                    if i == j and ti == tj:
                        row_ids = lax.broadcasted_iota(jnp.int32, (TILE, TILE), 0)
                        col_ids = lax.broadcasted_iota(jnp.int32, (TILE, TILE), 1)
                        part = jnp.where(row_ids == col_ids, NEG_BIG, part)
                    scores.append(part)
            top = functools.reduce(jnp.maximum, scores)
            top = jnp.max(top, axis=1, keepdims=True)
            expd = [jnp.exp(part - top) for part in scores]
            here = slice(i * rows + ti * TILE, i * rows + (ti + 1) * TILE)
            total_ref[here, :] = jnp.sum(functools.reduce(jnp.add, expd), axis=1, keepdims=True)
            for k, part in enumerate(expd):
                weight_ref[here, k * TILE : (k + 1) * TILE] = part.astype(jnp.bfloat16)


def weigh(edges, bias, mine, theirs):
    nodes = 2 * mine.shape[0]
    return pl.pallas_call(
        weigh_kernel,
        out_shape=[
            jax.ShapeDtypeStruct((nodes, nodes), jnp.bfloat16),
            jax.ShapeDtypeStruct((nodes, 1), jnp.float32),
        ],
        in_specs=[smem_spec()] * 2 + [vmem_spec()] * 2,
        out_specs=[vmem_spec()] * 2,
        compiler_params=pltpu.CompilerParams(vmem_limit_bytes=16 * 2**20),
        cost_estimate=pl.CostEstimate(
            flops=2 * nodes * nodes * DH, bytes_accessed=2 * nodes * nodes, transcendentals=nodes * nodes
        ),
        name="weigh",
    )(edges, bias, mine, theirs)


def average_kernel(blocks, weight_ref, total_ref, mine_ref, theirs_ref, *outs):
    rows = mine_ref.shape[0] // 2
    held = (mine_ref, theirs_ref)
    for out_ref, i in zip(outs, blocks):
        here = slice(i * rows, (i + 1) * rows)
        mixed = None
        for j in range(4):
            term = jnp.dot(
                weight_ref[here, j * rows : (j + 1) * rows],
                held[j % 2][j // 2 * rows : (j // 2 + 1) * rows, :],
                preferred_element_type=jnp.float32,
            )
            mixed = term if mixed is None else mixed + term
        out_ref[...] = (mixed / total_ref[here, :]).astype(jnp.bfloat16)


def average(blocks, weights, total, mine, theirs):
    rows = mine.shape[0] // 2
    return pl.pallas_call(
        functools.partial(average_kernel, blocks),
        out_shape=[jax.ShapeDtypeStruct((rows, DH), jnp.bfloat16)] * len(blocks),
        in_specs=[vmem_spec()] * 4,
        out_specs=[vmem_spec()] * len(blocks),
        compiler_params=pltpu.CompilerParams(vmem_limit_bytes=16 * 2**20),
        cost_estimate=pl.CostEstimate(
            flops=8 * len(blocks) * rows * rows * DH, bytes_accessed=weights.size, transcendentals=0
        ),
        name="average",
    )(weights, total, mine, theirs)


def emit_kernel(counts, *refs):
    parts, refs = refs[:4], refs[4:]
    weights = []
    for count in counts:
        weights.append(refs[:count])
        refs = refs[count:]
    outs, heads, terms = refs[:8], refs[8], refs[9]
    node, head = lax.axis_index("node"), lax.axis_index("head")
    far, near = head // 2, head % 2
    for i in range(4):
        heads[node ^ i] = parts[i][...]
    attn = jnp.concatenate([heads[i] for i in range(4)], axis=1)
    width = outs[0].shape[1]
    for i in range(4):
        plane = node ^ i ^ far
        for side in range(2):
            start = pl.multiple_of((near ^ side) * width, width)
            total, first = None, 0
            for ref in weights[i]:
                last = first + ref.shape[0]
                term = jnp.dot(
                    attn[:, first:last], ref[:, pl.ds(start, width)],
                    preferred_element_type=jnp.float32,
                )
                total, first = term if total is None else total + term, last
            terms[4 * side + plane] = total.astype(jnp.bfloat16)
    for i in range(8):
        outs[i][...] = terms[i]


def emit(parts, weights):
    rows = parts[0].shape[0]
    depth, cols = weights[0][0].shape
    counts = [len(pieces) for pieces in weights]
    flops = 2 * rows * depth * 4 * cols
    moved = 2 * (rows * depth + 4 * depth * cols + 4 * rows * cols)
    return pl.pallas_call(
        functools.partial(emit_kernel, counts),
        out_shape=[jax.ShapeDtypeStruct((rows, cols // 2), jnp.bfloat16)] * 8,
        in_specs=[vmem_spec()] * (4 + sum(counts)),
        out_specs=[vmem_spec()] * 8,
        scratch_shapes=[
            pltpu.VMEM((4, rows, DH), jnp.bfloat16),
            pltpu.VMEM((8, rows, cols // 2), jnp.bfloat16),
        ],
        compiler_params=pltpu.CompilerParams(vmem_limit_bytes=20 * 2**20),
        cost_estimate=pl.CostEstimate(flops=flops, bytes_accessed=moved, transcendentals=0),
        name="emit",
    )(*parts, *[piece for pieces in weights for piece in pieces])


def one_head_each(node_feats, w_qk, w_val, w_out, edge_types, rel_bias):
    depth, rows = w_out.shape[0], node_feats.shape[0]
    across = functools.partial(swap, axis="node", mask=2)
    beside = functools.partial(swap, axis="node", mask=1)
    along = functools.partial(swap, axis="head", mask=1)

    edges = [edge_types] + [swap(edge_types, "node", i) for i in range(1, 4)]
    far = {i: swap(node_feats, "head", 2 * i) for i in (3, 2, 1)}
    out_first = across(after(w_out[: depth // 2], *edges))
    edges = jnp.stack(edges)
    keep_0, send_0 = sort(node_feats, far[3], 1, 1)
    moved_0, keep_0y = [across(send_0[0])], [along(keep_0[0])]
    out_second = across(after(w_out[depth // 2 : 3 * depth // 4], moved_0[0], out_first))
    moved_0y = [along(moved_0[0])]
    close, distant = lax.optimization_barrier((far[1], far[2], keep_0y[0]))[:2]
    keep_1, send_1 = sort(close, distant, 1, 1)
    moved_1 = [across(part) for part in send_1]
    keep_1y = [along(keep_1[0])]
    moved_1y = [along(part) for part in moved_1]
    out_third = across(after(w_out[3 * depth // 4 :], moved_1[-1], out_second))
    qk_beside, val_beside = beside(w_qk), beside(w_val)
    qk_beside = after(qk_beside, out_first)
    pieces = [keep_0, keep_0y, keep_1, keep_1y, moved_0, moved_0y, moved_1, moved_1y]

    qk_keep, qk_send = project(pieces, [w_qk, qk_beside])
    qk_moved = across(qk_send)
    val_keep, val_send = project(pieces, [w_val, val_beside])
    val_moved = across(val_send)
    qk_mine, qk_give = combine(qk_keep, after(qk_moved, val_send, out_third))
    weights, total = weigh(edges, rel_bias.T, qk_mine, beside(qk_give))
    val_mine, val_give = combine(val_keep, after(val_moved, total))
    attn = average((0, 1, 2, 3), weights, total, val_mine, beside(val_give))
    attn = [attn[0]] + [swap(attn[i], "node", i) for i in range(1, 4)]

    out_across = [out_first, out_second, out_third]
    out_beside = beside(after(w_out, moved_1[0]))
    out_diagonal = [beside(after(piece, moved_1[0])) for piece in out_across[:2]] + [beside(out_third)]
    terms = emit(attn, [[w_out], [out_beside], out_across, out_diagonal])

    def pair(mine, send):
        return mine.astype(jnp.float32) + along(send).astype(jnp.float32)

    pair_3 = pair(terms[3], terms[7]).astype(jnp.bfloat16)
    pair_2 = pair(terms[2], terms[6]).astype(jnp.bfloat16)
    pair_1 = pair(terms[1], after(terms[5], pair_3)).astype(jnp.bfloat16)
    total = pair(terms[0], after(terms[4], pair_2))
    for i, part in ((3, pair_3), (2, pair_2), (1, pair_1)):
        total = total + swap(part, "head", 2 * i).astype(jnp.float32)
    return total.astype(jnp.bfloat16)


def from_behind(value, axis, by):
    peers = lax.axis_size(axis)
    return lax.ppermute(value, axis, [(i, (i + by) % peers) for i in range(peers)])


def pair_scores(queries, key_rows):
    inv_root = 1.0 / DH**0.5
    return (
        jnp.einsum("qhd,khd->hqk", queries, key_rows, preferred_element_type=jnp.float32) * inv_root
    )


def update(carried, scaled, bias_cols, value_rows, self_mask):
    head_count, query_count, key_count = scaled.shape
    tiles = bias_cols.shape[1]
    biased = (
        scaled.reshape(head_count, tiles, query_count // tiles, key_count)
        + bias_cols[:, :, None, :]
    )
    biased = biased.reshape(head_count, query_count, key_count)
    if self_mask is not None:
        biased = jnp.where(self_mask[None], NEG_BIG, biased)
    top_old, total_old, accum_old = carried
    top_new = jnp.maximum(top_old, jnp.max(biased, axis=2))
    expd = jnp.exp(biased - top_new[:, :, None])
    if self_mask is not None:
        expd = jnp.where(self_mask[None], 0.0, expd)
    factor = jnp.exp(top_old - top_new)
    total_new = total_old * factor + jnp.sum(expd, axis=2)
    product = jnp.einsum(
        "hqk,khd->hqd", expd.astype(jnp.bfloat16), value_rows, preferred_element_type=jnp.float32
    )
    return (top_new, total_new, accum_old * factor[:, :, None] + product)


def on_device(node_feats, w_qk, w_val, w_out, edge_types, rel_bias):
    row_count = node_feats.shape[0]
    col_width = w_qk.shape[1]
    head_count = rel_bias.shape[1]
    tile_rows = edge_types.shape[0]
    full_qk, full_val = (
        lax.all_gather(w_qk, "node", axis=0, tiled=True),
        lax.all_gather(w_val, "node", axis=0, tiled=True),
    )
    shard_piece = lax.all_gather(node_feats, "head", axis=1, tiled=True)
    proj_qk = jnp.dot(shard_piece, full_qk, preferred_element_type=jnp.float32)
    proj_val = jnp.dot(shard_piece, full_val, preferred_element_type=jnp.float32)
    qk_local = proj_qk.astype(jnp.bfloat16)
    val_local = proj_val.astype(jnp.bfloat16)
    queries = qk_local.reshape(row_count, head_count, DH)
    values = val_local.reshape(row_count, head_count, DH)
    relation_ids = jnp.arange(rel_bias.shape[0], dtype=jnp.int32)
    one_hot = (edge_types[:, :, None] == relation_ids[None, None, :]).astype(jnp.float32)
    tile_bias = jnp.einsum("abr,rh->hab", one_hot, rel_bias, precision=lax.Precision.HIGHEST)
    expanded = jnp.repeat(tile_bias, TILE, axis=2)
    my_block = lax.axis_index("node")
    first_row = my_block * row_count
    row_ids = first_row + jnp.arange(row_count, dtype=jnp.int32)
    initial = (
        jnp.full((head_count, row_count), NEG_BIG, jnp.float32),
        jnp.zeros((head_count, row_count), jnp.float32),
        jnp.zeros((head_count, row_count, DH), jnp.float32),
    )
    node_count = lax.axis_size("node")
    rounds = node_count // 2
    own_cols = lax.dynamic_slice_in_dim(expanded, first_row, row_count, 2)
    own_mask = row_ids[:, None] == row_ids[None, :]
    own_state = update(initial, pair_scores(queries, queries), own_cols, values, own_mask)

    def one_round(round_no, carried):
        mine, moving_block, moving_state = carried
        key_flat, value_flat = from_behind((moving_block[0], moving_block[1]), "node", 1)
        bias_moved, top_moved, total_moved, accum_moved = (
            from_behind(moving_state[0].astype(jnp.bfloat16), "node", 1).astype(jnp.float32),
            from_behind(moving_state[1].astype(jnp.bfloat16), "node", 1).astype(jnp.float32),
            from_behind(moving_state[2].astype(jnp.bfloat16), "node", 1).astype(jnp.float32),
            from_behind(moving_state[3].astype(jnp.bfloat16), "node", 1).astype(jnp.float32),
        )
        partner = (my_block - round_no) % node_count
        key_rows = key_flat.reshape(row_count, head_count, DH)
        value_rows = value_flat.reshape(row_count, head_count, DH)
        raw_scores = pair_scores(queries, key_rows)
        mine_cols = lax.dynamic_slice_in_dim(expanded, partner * row_count, row_count, 2)
        mine = update(mine, raw_scores, mine_cols, value_rows, None)
        back_tiles = lax.dynamic_slice_in_dim(bias_moved, my_block * tile_rows, tile_rows, 2)
        back_cols = jnp.repeat(back_tiles, TILE, axis=2)
        passed = update(
            (top_moved, total_moved, accum_moved),
            jnp.transpose(raw_scores, (0, 2, 1)),
            back_cols,
            values,
            None,
        )
        keep_flag = 2 * round_no != node_count
        kept = jax.tree.map(
            lambda fresh, stale: jnp.where(keep_flag, fresh, stale),
            passed,
            (top_moved, total_moved, accum_moved),
        )
        return (mine, (key_flat, value_flat), (bias_moved, kept[0], kept[1], kept[2]))

    start_state = (tile_bias, initial[0], initial[1], initial[2])
    own_state, _, final_moving = lax.fori_loop(
        1, rounds + 1, one_round, (own_state, (qk_local, val_local), start_state)
    )
    top_home, total_home, accum_home = (
        from_behind(final_moving[1].astype(jnp.bfloat16), "node", -rounds).astype(jnp.float32),
        from_behind(final_moving[2].astype(jnp.bfloat16), "node", -rounds).astype(jnp.float32),
        from_behind(final_moving[3].astype(jnp.bfloat16), "node", -rounds).astype(jnp.float32),
    )
    top_fin = jnp.maximum(own_state[0], top_home)
    factor_own = jnp.exp(own_state[0] - top_fin)
    factor_home = jnp.exp(top_home - top_fin)
    total_fin = own_state[1] * factor_own + total_home * factor_home
    accum_fin = own_state[2] * factor_own[:, :, None] + accum_home * factor_home[:, :, None]
    attn_heads = (accum_fin / total_fin[:, :, None]).astype(jnp.bfloat16)
    attn = jnp.transpose(attn_heads, (1, 0, 2)).reshape(row_count, col_width)
    terms = jnp.dot(
        attn, lax.all_gather(w_out, "node", axis=1, tiled=True), preferred_element_type=jnp.float32
    )
    return lax.psum_scatter(terms.astype(jnp.bfloat16), "head", scatter_dimension=1, tiled=True)

def solution(mesh):
    in_specs = (
        P("node", "head"),
        P("node", "head"),
        P("node", "head"),
        P("head", "node"),
        P("node", None),
        P(None, "head"),
    )
    out_specs = P("node", "head")

    def whole(node_feats, w_qk, w_val, w_out, edge_types, rel_bias):
        node_count, head_count = mesh.shape["node"], mesh.shape["head"]
        column_heads = rel_bias.shape[1] // head_count
        fits = (
            node_count == 4
            and head_count == 2 * node_count
            and column_heads == node_count
            and node_feats.shape[0] % (node_count * TILE) == 0
        )
        body = one_head_each if fits else on_device
        mapped = jax.shard_map(
            body, mesh=mesh, in_specs=in_specs, out_specs=out_specs, check_vma=False
        )
        return mapped(node_feats, w_qk, w_val, w_out, edge_types, rel_bias)

    return whole
```

```python
import functools

import jax
import jax.numpy as jnp
from jax import lax
from jax.experimental import pallas as pl
from jax.experimental.pallas import tpu as pltpu
from jax.sharding import PartitionSpec as P

DH = 128
TILE = 128


NEG_BIG = -1e30


def swap(value, axis, mask):
    peers = lax.axis_size(axis)
    return lax.ppermute(value, axis, [(i, i ^ mask) for i in range(peers)])


def after(value, *others):
    return lax.optimization_barrier((value, *others))[0]


def vmem_spec():
    return pl.BlockSpec(memory_space=pltpu.VMEM)


def smem_spec():
    return pl.BlockSpec(memory_space=pltpu.SMEM)


def in_line(node, head):
    return node // 2 == head // 4


def sort_kernel(keeps, close_ref, distant_ref, *outs):
    lined = in_line(lax.axis_index("node"), lax.axis_index("head"))

    def place(send_ref, keep_ref):
        for ref, parts in ((keep_ref, outs[:keeps]), (send_ref, outs[keeps:])):
            start = 0
            for part in parts:
                part[...] = ref[start : start + part.shape[0], :]
                start += part.shape[0]

    @pl.when(lined)
    def _():
        place(distant_ref, close_ref)

    @pl.when(jnp.logical_not(lined))
    def _():
        place(close_ref, distant_ref)


def sort(close, distant, keeps, sends):
    rows, cols = close.shape
    shapes = [
        jax.ShapeDtypeStruct((rows // parts, cols), close.dtype)
        for parts in (keeps, sends)
        for _ in range(parts)
    ]
    outs = pl.pallas_call(
        functools.partial(sort_kernel, keeps),
        out_shape=shapes,
        in_specs=[vmem_spec()] * 2,
        out_specs=[vmem_spec()] * len(shapes),
        compiler_params=pltpu.CompilerParams(vmem_limit_bytes=8 * 2**20),
        cost_estimate=pl.CostEstimate(flops=0, bytes_accessed=8 * close.size, transcendentals=0),
        name="sort",
    )(close, distant)
    return outs[:keeps], outs[keeps:]


def project_kernel(counts, *refs):
    pieces = []
    for count in counts:
        pieces.append(refs[:count])
        refs = refs[count:]
    weights, (keep_ref, send_ref, total) = refs[:2], refs[2:]
    node, head = lax.axis_index("node"), lax.axis_index("head")
    side, core = node // 2, node % 2
    slot = (head // 2) % 2 ^ jnp.where(in_line(node, head), 0, 1)
    near = head % 2
    rows, depth = sum(ref.shape[0] for ref in pieces[0]), pieces[0][0].shape[1]
    width = keep_ref.shape[1]
    mine = pl.ds(pl.multiple_of(side * width, width), width)
    theirs = pl.ds(pl.multiple_of((1 - side) * width, width), width)

    def piece(block, plane, other):
        held = pieces[4 * block + 2 * plane + other]
        return jnp.concatenate([ref[...] for ref in held], axis=0)

    def work(flip):
        for block in range(2):
            out = slice(block * rows, (block + 1) * rows)
            sum_so_far = None
            for plane in range(2):
                for other in range(2):
                    start = pl.multiple_of((near ^ other) * depth, depth)
                    term = jnp.dot(
                        piece(block, plane, other),
                        weights[plane ^ flip][pl.ds(start, depth), :],
                        preferred_element_type=jnp.float32,
                    )
                    sum_so_far = term if sum_so_far is None else sum_so_far + term
            total[...] = sum_so_far
            keep_ref[out, :] = total[:, mine]
            send_ref[out, :] = total[:, theirs].astype(jnp.bfloat16)

    for flip in range(2):
        pl.when(slot ^ core == flip)(functools.partial(work, flip))


def project(pieces, weights):
    rows, depth = sum(ref.shape[0] for ref in pieces[0]), pieces[0][0].shape[1]
    cols = weights[0].shape[1]
    counts = [len(held) for held in pieces]
    flops = 2 * 2 * rows * 4 * depth * cols
    moved = 2 * (8 * rows * depth + 4 * depth * cols + 3 * rows * cols)
    return pl.pallas_call(
        functools.partial(project_kernel, counts),
        out_shape=[
            jax.ShapeDtypeStruct((2 * rows, cols // 2), jnp.float32),
            jax.ShapeDtypeStruct((2 * rows, cols // 2), jnp.bfloat16),
        ],
        in_specs=[vmem_spec()] * (sum(counts) + 2),
        out_specs=[vmem_spec()] * 2,
        scratch_shapes=[pltpu.VMEM((rows, cols), jnp.float32)],
        compiler_params=pltpu.CompilerParams(vmem_limit_bytes=20 * 2**20),
        cost_estimate=pl.CostEstimate(flops=flops, bytes_accessed=moved, transcendentals=0),
        name="project",
    )(*[piece for held in pieces for piece in held], *weights)


def combine_kernel(keep_ref, moved_ref, mine_ref, give_ref):
    core = lax.axis_index("node") % 2
    rows = keep_ref.shape[0] // 2
    for out_ref, place in ((mine_ref, core), (give_ref, 1 - core)):
        cols = pl.ds(pl.multiple_of(place * DH, DH), DH)
        for block in range(2):
            here = slice(block * rows, (block + 1) * rows)
            there = slice((1 - block) * rows, (2 - block) * rows)
            both = keep_ref[here, cols] + moved_ref[there, cols].astype(jnp.float32)
            out_ref[here, :] = both.astype(jnp.bfloat16)


def combine(keep, moved):
    shape = jax.ShapeDtypeStruct((keep.shape[0], DH), jnp.bfloat16)
    return pl.pallas_call(
        combine_kernel,
        out_shape=[shape, shape],
        in_specs=[vmem_spec()] * 2,
        out_specs=[vmem_spec()] * 2,
        compiler_params=pltpu.CompilerParams(vmem_limit_bytes=8 * 2**20),
        cost_estimate=pl.CostEstimate(flops=keep.size, bytes_accessed=8 * keep.size, transcendentals=0),
        name="combine",
    )(keep, moved)


def weigh_kernel(edge_ref, bias_ref, mine_ref, theirs_ref, weight_ref, total_ref):
    node = lax.axis_index("node")
    inv_root = 1.0 / DH**0.5
    rows = mine_ref.shape[0] // 2
    tiles = rows // TILE
    held = (mine_ref, theirs_ref)
    for i in range(4):
        for ti in range(tiles):
            base = i // 2 * rows + ti * TILE
            queries = held[i % 2][base : base + TILE, :]
            scores = []
            for j in range(4):
                keys = held[j % 2][j // 2 * rows : (j // 2 + 1) * rows, :]
                raw = lax.dot_general(
                    queries, keys, (((1,), (1,)), ((), ())), preferred_element_type=jnp.float32
                )
                for tj in range(tiles):
                    relation = edge_ref[i, ti, tiles * (node ^ j) + tj]
                    part = raw[:, tj * TILE : (tj + 1) * TILE] * inv_root + bias_ref[node, relation]
                    if i == j and ti == tj:
                        row_ids = lax.broadcasted_iota(jnp.int32, (TILE, TILE), 0)
                        col_ids = lax.broadcasted_iota(jnp.int32, (TILE, TILE), 1)
                        part = jnp.where(row_ids == col_ids, NEG_BIG, part)
                    scores.append(part)
            top = functools.reduce(jnp.maximum, scores)
            top = jnp.max(top, axis=1, keepdims=True)
            expd = [jnp.exp(part - top) for part in scores]
            here = slice(i * rows + ti * TILE, i * rows + (ti + 1) * TILE)
            total_ref[here, :] = jnp.sum(functools.reduce(jnp.add, expd), axis=1, keepdims=True)
            for k, part in enumerate(expd):
                weight_ref[here, k * TILE : (k + 1) * TILE] = part.astype(jnp.bfloat16)


def weigh(edges, bias, mine, theirs):
    nodes = 2 * mine.shape[0]
    return pl.pallas_call(
        weigh_kernel,
        out_shape=[
            jax.ShapeDtypeStruct((nodes, nodes), jnp.bfloat16),
            jax.ShapeDtypeStruct((nodes, 1), jnp.float32),
        ],
        in_specs=[smem_spec()] * 2 + [vmem_spec()] * 2,
        out_specs=[vmem_spec()] * 2,
        compiler_params=pltpu.CompilerParams(vmem_limit_bytes=16 * 2**20),
        cost_estimate=pl.CostEstimate(
            flops=2 * nodes * nodes * DH, bytes_accessed=2 * nodes * nodes, transcendentals=nodes * nodes
        ),
        name="weigh",
    )(edges, bias, mine, theirs)


def average_kernel(blocks, weight_ref, total_ref, mine_ref, theirs_ref, *outs):
    rows = mine_ref.shape[0] // 2
    held = (mine_ref, theirs_ref)
    for out_ref, i in zip(outs, blocks):
        here = slice(i * rows, (i + 1) * rows)
        mixed = None
        for j in range(4):
            term = jnp.dot(
                weight_ref[here, j * rows : (j + 1) * rows],
                held[j % 2][j // 2 * rows : (j // 2 + 1) * rows, :],
                preferred_element_type=jnp.float32,
            )
            mixed = term if mixed is None else mixed + term
        out_ref[...] = (mixed / total_ref[here, :]).astype(jnp.bfloat16)


def average(blocks, weights, total, mine, theirs):
    rows = mine.shape[0] // 2
    return pl.pallas_call(
        functools.partial(average_kernel, blocks),
        out_shape=[jax.ShapeDtypeStruct((rows, DH), jnp.bfloat16)] * len(blocks),
        in_specs=[vmem_spec()] * 4,
        out_specs=[vmem_spec()] * len(blocks),
        compiler_params=pltpu.CompilerParams(vmem_limit_bytes=16 * 2**20),
        cost_estimate=pl.CostEstimate(
            flops=8 * len(blocks) * rows * rows * DH, bytes_accessed=weights.size, transcendentals=0
        ),
        name="average",
    )(weights, total, mine, theirs)


def unpack(counts, refs):
    parts, refs = refs[:4], refs[4:]
    weights = []
    for count in counts:
        weights.append(refs[:count])
        refs = refs[count:]
    return parts, weights, refs


def gather_heads(parts, heads):
    node = lax.axis_index("node")
    for i in range(4):
        heads[node ^ i] = parts[i][...]
    return jnp.concatenate([heads[i] for i in range(4)], axis=1)


def product(attn, held, start, width):
    total, first = None, 0
    for ref in held:
        last = first + ref.shape[0]
        term = jnp.dot(
            attn[:, first:last], ref[:, pl.ds(start, width)], preferred_element_type=jnp.float32
        )
        total, first = term if total is None else total + term, last
    return total.astype(jnp.bfloat16)


def lead_kernel(counts, *refs):
    parts, weights, (out_ref, heads) = unpack(counts, refs)
    node, head = lax.axis_index("node"), lax.axis_index("head")
    attn = gather_heads(parts, heads)
    width = out_ref.shape[1]
    start = pl.multiple_of((head % 2 ^ 1) * width, width)

    def work(i):
        out_ref[...] = product(attn, weights[i], start, width)

    for i in range(4):
        pl.when(node ^ i ^ (head // 2) == 3)(functools.partial(work, i))


def emit_kernel(counts, *refs):
    parts, weights, refs = unpack(counts, refs)
    outs, heads, terms = refs[:7], refs[7], refs[8]
    node, head = lax.axis_index("node"), lax.axis_index("head")
    far, near = head // 2, head % 2
    attn = gather_heads(parts, heads)
    width = outs[0].shape[1]
    for i in range(4):
        for side in range(2):
            start = pl.multiple_of((near ^ side) * width, width)
            terms[4 * side + (node ^ i ^ far)] = product(attn, weights[i], start, width)
    for i in range(7):
        outs[i][...] = terms[i]


def lead(parts, weights):
    rows = parts[0].shape[0]
    depth, cols = weights[0][0].shape
    counts = [len(pieces) for pieces in weights]
    return pl.pallas_call(
        functools.partial(lead_kernel, counts),
        out_shape=jax.ShapeDtypeStruct((rows, cols // 2), jnp.bfloat16),
        in_specs=[vmem_spec()] * (4 + sum(counts)),
        out_specs=vmem_spec(),
        scratch_shapes=[pltpu.VMEM((4, rows, DH), jnp.bfloat16)],
        compiler_params=pltpu.CompilerParams(vmem_limit_bytes=16 * 2**20),
        cost_estimate=pl.CostEstimate(
            flops=rows * depth * cols, bytes_accessed=depth * cols, transcendentals=0
        ),
        name="lead",
    )(*parts, *[piece for pieces in weights for piece in pieces])


def emit(parts, weights):
    rows = parts[0].shape[0]
    depth, cols = weights[0][0].shape
    counts = [len(pieces) for pieces in weights]
    flops = 2 * rows * depth * 4 * cols
    moved = 2 * (rows * depth + 4 * depth * cols + 4 * rows * cols)
    return pl.pallas_call(
        functools.partial(emit_kernel, counts),
        out_shape=[jax.ShapeDtypeStruct((rows, cols // 2), jnp.bfloat16)] * 7,
        in_specs=[vmem_spec()] * (4 + sum(counts)),
        out_specs=[vmem_spec()] * 7,
        scratch_shapes=[
            pltpu.VMEM((4, rows, DH), jnp.bfloat16),
            pltpu.VMEM((8, rows, cols // 2), jnp.bfloat16),
        ],
        compiler_params=pltpu.CompilerParams(vmem_limit_bytes=20 * 2**20),
        cost_estimate=pl.CostEstimate(flops=flops, bytes_accessed=moved, transcendentals=0),
        name="emit",
    )(*parts, *[piece for pieces in weights for piece in pieces])


def one_head_each(node_feats, w_qk, w_val, w_out, edge_types, rel_bias):
    depth, rows = w_out.shape[0], node_feats.shape[0]
    across = functools.partial(swap, axis="node", mask=2)
    beside = functools.partial(swap, axis="node", mask=1)
    along = functools.partial(swap, axis="head", mask=1)

    edges = [edge_types] + [swap(edge_types, "node", i) for i in range(1, 4)]
    far = {i: swap(node_feats, "head", 2 * i) for i in (3, 2, 1)}
    out_first = across(after(w_out[: depth // 2], *edges))
    edges = jnp.stack(edges)
    keep_0, send_0 = sort(node_feats, far[3], 1, 1)
    moved_0, keep_0y = [across(send_0[0])], [along(keep_0[0])]
    out_second = across(after(w_out[depth // 2 : 3 * depth // 4], moved_0[0], out_first))
    moved_0y = [along(moved_0[0])]
    close, distant = lax.optimization_barrier((far[1], far[2], keep_0y[0]))[:2]
    keep_1, send_1 = sort(close, distant, 1, 1)
    moved_1 = [across(part) for part in send_1]
    keep_1y = [along(keep_1[0])]
    moved_1y = [along(part) for part in moved_1]
    out_third = across(after(w_out[3 * depth // 4 :], moved_1[-1], out_second))
    qk_beside, val_beside = beside(w_qk), beside(w_val)

    pieces = [keep_0, keep_0y, keep_1, keep_1y, moved_0, moved_0y, moved_1, moved_1y]

    qk_keep, qk_send = project(pieces, [w_qk, qk_beside])
    qk_moved = across(qk_send)
    val_keep, val_send = project(pieces, [w_val, val_beside])
    val_moved = across(val_send)
    qk_mine, qk_give = combine(qk_keep, after(qk_moved, val_send, out_third))
    weights, total = weigh(edges, rel_bias.T, qk_mine, beside(qk_give))
    val_mine, val_give = combine(val_keep, after(val_moved, total))
    attn = average((0, 1, 2, 3), weights, total, val_mine, beside(val_give))
    attn = [attn[0]] + [swap(attn[i], "node", i) for i in range(1, 4)]

    out_across = [out_first, out_second, out_third]
    out_beside = beside(after(w_out, moved_1[0]))
    out_diagonal = [beside(after(piece, moved_1[0])) for piece in out_across[:2]] + [beside(out_third)]
    first_send = lead(attn, [[w_out], [out_beside], out_across, out_diagonal])
    terms = emit(attn, [[w_out], [out_beside], out_across, out_diagonal])

    def pair(mine, send):
        return mine.astype(jnp.float32) + along(send).astype(jnp.float32)

    pair_3 = pair(terms[3], first_send).astype(jnp.bfloat16)
    pair_2 = pair(terms[2], terms[6]).astype(jnp.bfloat16)
    pair_1 = pair(terms[1], after(terms[5], pair_3)).astype(jnp.bfloat16)
    total = pair(terms[0], after(terms[4], pair_2))
    for i, part in ((3, pair_3), (2, pair_2), (1, pair_1)):
        total = total + swap(part, "head", 2 * i).astype(jnp.float32)
    return total.astype(jnp.bfloat16)


def from_behind(value, axis, by):
    peers = lax.axis_size(axis)
    return lax.ppermute(value, axis, [(i, (i + by) % peers) for i in range(peers)])


def pair_scores(queries, key_rows):
    inv_root = 1.0 / DH**0.5
    return (
        jnp.einsum("qhd,khd->hqk", queries, key_rows, preferred_element_type=jnp.float32) * inv_root
    )


def update(carried, scaled, bias_cols, value_rows, self_mask):
    head_count, query_count, key_count = scaled.shape
    tiles = bias_cols.shape[1]
    biased = (
        scaled.reshape(head_count, tiles, query_count // tiles, key_count)
        + bias_cols[:, :, None, :]
    )
    biased = biased.reshape(head_count, query_count, key_count)
    if self_mask is not None:
        biased = jnp.where(self_mask[None], NEG_BIG, biased)
    top_old, total_old, accum_old = carried
    top_new = jnp.maximum(top_old, jnp.max(biased, axis=2))
    expd = jnp.exp(biased - top_new[:, :, None])
    if self_mask is not None:
        expd = jnp.where(self_mask[None], 0.0, expd)
    factor = jnp.exp(top_old - top_new)
    total_new = total_old * factor + jnp.sum(expd, axis=2)
    product = jnp.einsum(
        "hqk,khd->hqd", expd.astype(jnp.bfloat16), value_rows, preferred_element_type=jnp.float32
    )
    return (top_new, total_new, accum_old * factor[:, :, None] + product)


def on_device(node_feats, w_qk, w_val, w_out, edge_types, rel_bias):
    row_count = node_feats.shape[0]
    col_width = w_qk.shape[1]
    head_count = rel_bias.shape[1]
    tile_rows = edge_types.shape[0]
    full_qk, full_val = (
        lax.all_gather(w_qk, "node", axis=0, tiled=True),
        lax.all_gather(w_val, "node", axis=0, tiled=True),
    )
    shard_piece = lax.all_gather(node_feats, "head", axis=1, tiled=True)
    proj_qk = jnp.dot(shard_piece, full_qk, preferred_element_type=jnp.float32)
    proj_val = jnp.dot(shard_piece, full_val, preferred_element_type=jnp.float32)
    qk_local = proj_qk.astype(jnp.bfloat16)
    val_local = proj_val.astype(jnp.bfloat16)
    queries = qk_local.reshape(row_count, head_count, DH)
    values = val_local.reshape(row_count, head_count, DH)
    relation_ids = jnp.arange(rel_bias.shape[0], dtype=jnp.int32)
    one_hot = (edge_types[:, :, None] == relation_ids[None, None, :]).astype(jnp.float32)
    tile_bias = jnp.einsum("abr,rh->hab", one_hot, rel_bias, precision=lax.Precision.HIGHEST)
    expanded = jnp.repeat(tile_bias, TILE, axis=2)
    my_block = lax.axis_index("node")
    first_row = my_block * row_count
    row_ids = first_row + jnp.arange(row_count, dtype=jnp.int32)
    initial = (
        jnp.full((head_count, row_count), NEG_BIG, jnp.float32),
        jnp.zeros((head_count, row_count), jnp.float32),
        jnp.zeros((head_count, row_count, DH), jnp.float32),
    )
    node_count = lax.axis_size("node")
    rounds = node_count // 2
    own_cols = lax.dynamic_slice_in_dim(expanded, first_row, row_count, 2)
    own_mask = row_ids[:, None] == row_ids[None, :]
    own_state = update(initial, pair_scores(queries, queries), own_cols, values, own_mask)

    def one_round(round_no, carried):
        mine, moving_block, moving_state = carried
        key_flat, value_flat = from_behind((moving_block[0], moving_block[1]), "node", 1)
        bias_moved, top_moved, total_moved, accum_moved = (
            from_behind(moving_state[0].astype(jnp.bfloat16), "node", 1).astype(jnp.float32),
            from_behind(moving_state[1].astype(jnp.bfloat16), "node", 1).astype(jnp.float32),
            from_behind(moving_state[2].astype(jnp.bfloat16), "node", 1).astype(jnp.float32),
            from_behind(moving_state[3].astype(jnp.bfloat16), "node", 1).astype(jnp.float32),
        )
        partner = (my_block - round_no) % node_count
        key_rows = key_flat.reshape(row_count, head_count, DH)
        value_rows = value_flat.reshape(row_count, head_count, DH)
        raw_scores = pair_scores(queries, key_rows)
        mine_cols = lax.dynamic_slice_in_dim(expanded, partner * row_count, row_count, 2)
        mine = update(mine, raw_scores, mine_cols, value_rows, None)
        back_tiles = lax.dynamic_slice_in_dim(bias_moved, my_block * tile_rows, tile_rows, 2)
        back_cols = jnp.repeat(back_tiles, TILE, axis=2)
        passed = update(
            (top_moved, total_moved, accum_moved),
            jnp.transpose(raw_scores, (0, 2, 1)),
            back_cols,
            values,
            None,
        )
        keep_flag = 2 * round_no != node_count
        kept = jax.tree.map(
            lambda fresh, stale: jnp.where(keep_flag, fresh, stale),
            passed,
            (top_moved, total_moved, accum_moved),
        )
        return (mine, (key_flat, value_flat), (bias_moved, kept[0], kept[1], kept[2]))

    start_state = (tile_bias, initial[0], initial[1], initial[2])
    own_state, _, final_moving = lax.fori_loop(
        1, rounds + 1, one_round, (own_state, (qk_local, val_local), start_state)
    )
    top_home, total_home, accum_home = (
        from_behind(final_moving[1].astype(jnp.bfloat16), "node", -rounds).astype(jnp.float32),
        from_behind(final_moving[2].astype(jnp.bfloat16), "node", -rounds).astype(jnp.float32),
        from_behind(final_moving[3].astype(jnp.bfloat16), "node", -rounds).astype(jnp.float32),
    )
    top_fin = jnp.maximum(own_state[0], top_home)
    factor_own = jnp.exp(own_state[0] - top_fin)
    factor_home = jnp.exp(top_home - top_fin)
    total_fin = own_state[1] * factor_own + total_home * factor_home
    accum_fin = own_state[2] * factor_own[:, :, None] + accum_home * factor_home[:, :, None]
    attn_heads = (accum_fin / total_fin[:, :, None]).astype(jnp.bfloat16)
    attn = jnp.transpose(attn_heads, (1, 0, 2)).reshape(row_count, col_width)
    terms = jnp.dot(
        attn, lax.all_gather(w_out, "node", axis=1, tiled=True), preferred_element_type=jnp.float32
    )
    return lax.psum_scatter(terms.astype(jnp.bfloat16), "head", scatter_dimension=1, tiled=True)

def solution(mesh):
    in_specs = (
        P("node", "head"),
        P("node", "head"),
        P("node", "head"),
        P("head", "node"),
        P("node", None),
        P(None, "head"),
    )
    out_specs = P("node", "head")

    def whole(node_feats, w_qk, w_val, w_out, edge_types, rel_bias):
        node_count, head_count = mesh.shape["node"], mesh.shape["head"]
        column_heads = rel_bias.shape[1] // head_count
        fits = (
            node_count == 4
            and head_count == 2 * node_count
            and column_heads == node_count
            and node_feats.shape[0] % (node_count * TILE) == 0
        )
        body = one_head_each if fits else on_device
        mapped = jax.shard_map(
            body, mesh=mesh, in_specs=in_specs, out_specs=out_specs, check_vma=False
        )
        return mapped(node_feats, w_qk, w_val, w_out, edge_types, rel_bias)

    return whole
```

```python
import functools

import jax
import jax.numpy as jnp
from jax import lax
from jax.experimental import pallas as pl
from jax.experimental.pallas import tpu as pltpu
from jax.sharding import PartitionSpec as P

DH = 128
TILE = 128


NEG_BIG = -1e30


def swap(value, axis, mask):
    peers = lax.axis_size(axis)
    return lax.ppermute(value, axis, [(i, i ^ mask) for i in range(peers)])


def after(value, *others):
    return lax.optimization_barrier((value, *others))[0]


def vmem_spec():
    return pl.BlockSpec(memory_space=pltpu.VMEM)


def smem_spec():
    return pl.BlockSpec(memory_space=pltpu.SMEM)


def in_line(node, head):
    return node // 2 == head // 4


def sort_kernel(keeps, close_ref, distant_ref, *outs):
    lined = in_line(lax.axis_index("node"), lax.axis_index("head"))

    def place(send_ref, keep_ref):
        for ref, parts in ((keep_ref, outs[:keeps]), (send_ref, outs[keeps:])):
            start = 0
            for part in parts:
                part[...] = ref[start : start + part.shape[0], :]
                start += part.shape[0]

    @pl.when(lined)
    def _():
        place(distant_ref, close_ref)

    @pl.when(jnp.logical_not(lined))
    def _():
        place(close_ref, distant_ref)


def sort(close, distant, keeps, sends):
    rows, cols = close.shape
    shapes = [
        jax.ShapeDtypeStruct((rows // parts, cols), close.dtype)
        for parts in (keeps, sends)
        for _ in range(parts)
    ]
    outs = pl.pallas_call(
        functools.partial(sort_kernel, keeps),
        out_shape=shapes,
        in_specs=[vmem_spec()] * 2,
        out_specs=[vmem_spec()] * len(shapes),
        compiler_params=pltpu.CompilerParams(vmem_limit_bytes=8 * 2**20),
        cost_estimate=pl.CostEstimate(flops=0, bytes_accessed=8 * close.size, transcendentals=0),
        name="sort",
    )(close, distant)
    return outs[:keeps], outs[keeps:]


def project_kernel(counts, *refs):
    pieces = []
    for count in counts:
        pieces.append(refs[:count])
        refs = refs[count:]
    weights, (keep_ref, send_ref, total) = refs[:2], refs[2:]
    node, head = lax.axis_index("node"), lax.axis_index("head")
    side, core = node // 2, node % 2
    slot = (head // 2) % 2 ^ jnp.where(in_line(node, head), 0, 1)
    near = head % 2
    rows, depth = sum(ref.shape[0] for ref in pieces[0]), pieces[0][0].shape[1]
    width = keep_ref.shape[1]
    mine = pl.ds(pl.multiple_of(side * width, width), width)
    theirs = pl.ds(pl.multiple_of((1 - side) * width, width), width)

    def piece(block, plane, other):
        held = pieces[4 * block + 2 * plane + other]
        return jnp.concatenate([ref[...] for ref in held], axis=0)

    def work(flip):
        for block in range(2):
            out = slice(block * rows, (block + 1) * rows)
            sum_so_far = None
            for plane in range(2):
                for other in range(2):
                    start = pl.multiple_of((near ^ other) * depth, depth)
                    term = jnp.dot(
                        piece(block, plane, other),
                        weights[plane ^ flip][pl.ds(start, depth), :],
                        preferred_element_type=jnp.float32,
                    )
                    sum_so_far = term if sum_so_far is None else sum_so_far + term
            total[...] = sum_so_far
            keep_ref[out, :] = total[:, mine]
            send_ref[out, :] = total[:, theirs].astype(jnp.bfloat16)

    for flip in range(2):
        pl.when(slot ^ core == flip)(functools.partial(work, flip))


def project(pieces, weights):
    rows, depth = sum(ref.shape[0] for ref in pieces[0]), pieces[0][0].shape[1]
    cols = weights[0].shape[1]
    counts = [len(held) for held in pieces]
    flops = 2 * 2 * rows * 4 * depth * cols
    moved = 2 * (8 * rows * depth + 4 * depth * cols + 3 * rows * cols)
    return pl.pallas_call(
        functools.partial(project_kernel, counts),
        out_shape=[
            jax.ShapeDtypeStruct((2 * rows, cols // 2), jnp.float32),
            jax.ShapeDtypeStruct((2 * rows, cols // 2), jnp.bfloat16),
        ],
        in_specs=[vmem_spec()] * (sum(counts) + 2),
        out_specs=[vmem_spec()] * 2,
        scratch_shapes=[pltpu.VMEM((rows, cols), jnp.float32)],
        compiler_params=pltpu.CompilerParams(vmem_limit_bytes=20 * 2**20),
        cost_estimate=pl.CostEstimate(flops=flops, bytes_accessed=moved, transcendentals=0),
        name="project",
    )(*[piece for held in pieces for piece in held], *weights)


def combine_kernel(keep_ref, moved_ref, mine_ref, give_ref):
    core = lax.axis_index("node") % 2
    rows = keep_ref.shape[0] // 2
    for out_ref, place in ((mine_ref, core), (give_ref, 1 - core)):
        cols = pl.ds(pl.multiple_of(place * DH, DH), DH)
        for block in range(2):
            here = slice(block * rows, (block + 1) * rows)
            there = slice((1 - block) * rows, (2 - block) * rows)
            both = keep_ref[here, cols] + moved_ref[there, cols].astype(jnp.float32)
            out_ref[here, :] = both.astype(jnp.bfloat16)


def combine(keep, moved):
    shape = jax.ShapeDtypeStruct((keep.shape[0], DH), jnp.bfloat16)
    return pl.pallas_call(
        combine_kernel,
        out_shape=[shape, shape],
        in_specs=[vmem_spec()] * 2,
        out_specs=[vmem_spec()] * 2,
        compiler_params=pltpu.CompilerParams(vmem_limit_bytes=8 * 2**20),
        cost_estimate=pl.CostEstimate(flops=keep.size, bytes_accessed=8 * keep.size, transcendentals=0),
        name="combine",
    )(keep, moved)


def weigh_kernel(edge_ref, bias_ref, mine_ref, theirs_ref, weight_ref, total_ref):
    node = lax.axis_index("node")
    inv_root = 1.0 / DH**0.5
    rows = mine_ref.shape[0] // 2
    tiles = rows // TILE
    held = (mine_ref, theirs_ref)
    for i in range(4):
        for ti in range(tiles):
            base = i // 2 * rows + ti * TILE
            queries = held[i % 2][base : base + TILE, :]
            scores = []
            for j in range(4):
                keys = held[j % 2][j // 2 * rows : (j // 2 + 1) * rows, :]
                raw = lax.dot_general(
                    queries, keys, (((1,), (1,)), ((), ())), preferred_element_type=jnp.float32
                )
                for tj in range(tiles):
                    relation = edge_ref[i, ti, tiles * (node ^ j) + tj]
                    part = raw[:, tj * TILE : (tj + 1) * TILE] * inv_root + bias_ref[node, relation]
                    if i == j and ti == tj:
                        row_ids = lax.broadcasted_iota(jnp.int32, (TILE, TILE), 0)
                        col_ids = lax.broadcasted_iota(jnp.int32, (TILE, TILE), 1)
                        part = jnp.where(row_ids == col_ids, NEG_BIG, part)
                    scores.append(part)
            top = functools.reduce(jnp.maximum, scores)
            top = jnp.max(top, axis=1, keepdims=True)
            expd = [jnp.exp(part - top) for part in scores]
            here = slice(i * rows + ti * TILE, i * rows + (ti + 1) * TILE)
            total_ref[here, :] = jnp.sum(functools.reduce(jnp.add, expd), axis=1, keepdims=True)
            for k, part in enumerate(expd):
                weight_ref[here, k * TILE : (k + 1) * TILE] = part.astype(jnp.bfloat16)


def weigh(edges, bias, mine, theirs):
    nodes = 2 * mine.shape[0]
    return pl.pallas_call(
        weigh_kernel,
        out_shape=[
            jax.ShapeDtypeStruct((nodes, nodes), jnp.bfloat16),
            jax.ShapeDtypeStruct((nodes, 1), jnp.float32),
        ],
        in_specs=[smem_spec()] * 2 + [vmem_spec()] * 2,
        out_specs=[vmem_spec()] * 2,
        compiler_params=pltpu.CompilerParams(vmem_limit_bytes=16 * 2**20),
        cost_estimate=pl.CostEstimate(
            flops=2 * nodes * nodes * DH, bytes_accessed=2 * nodes * nodes, transcendentals=nodes * nodes
        ),
        name="weigh",
    )(edges, bias, mine, theirs)


def average_kernel(blocks, weight_ref, total_ref, mine_ref, theirs_ref, *outs):
    rows = mine_ref.shape[0] // 2
    held = (mine_ref, theirs_ref)
    for out_ref, i in zip(outs, blocks):
        here = slice(i * rows, (i + 1) * rows)
        mixed = None
        for j in range(4):
            term = jnp.dot(
                weight_ref[here, j * rows : (j + 1) * rows],
                held[j % 2][j // 2 * rows : (j // 2 + 1) * rows, :],
                preferred_element_type=jnp.float32,
            )
            mixed = term if mixed is None else mixed + term
        out_ref[...] = (mixed / total_ref[here, :]).astype(jnp.bfloat16)


def average(blocks, weights, total, mine, theirs):
    rows = mine.shape[0] // 2
    return pl.pallas_call(
        functools.partial(average_kernel, blocks),
        out_shape=[jax.ShapeDtypeStruct((rows, DH), jnp.bfloat16)] * len(blocks),
        in_specs=[vmem_spec()] * 4,
        out_specs=[vmem_spec()] * len(blocks),
        compiler_params=pltpu.CompilerParams(vmem_limit_bytes=16 * 2**20),
        cost_estimate=pl.CostEstimate(
            flops=8 * len(blocks) * rows * rows * DH, bytes_accessed=weights.size, transcendentals=0
        ),
        name="average",
    )(weights, total, mine, theirs)


def unpack(counts, refs):
    parts, refs = refs[:4], refs[4:]
    weights = []
    for count in counts:
        weights.append(refs[:count])
        refs = refs[count:]
    return parts, weights, refs


def gather_heads(parts, heads):
    node = lax.axis_index("node")
    for i in range(4):
        heads[node ^ i] = parts[i][...]
    return jnp.concatenate([heads[i] for i in range(4)], axis=1)


def product(attn, held, start, width):
    total, first = None, 0
    for ref in held:
        last = first + ref.shape[0]
        term = jnp.dot(
            attn[:, first:last], ref[:, pl.ds(start, width)], preferred_element_type=jnp.float32
        )
        total, first = term if total is None else total + term, last
    return total.astype(jnp.bfloat16)


def lead_kernel(counts, *refs):
    parts, weights, (out_ref, heads) = unpack(counts, refs)
    node, head = lax.axis_index("node"), lax.axis_index("head")
    attn = gather_heads(parts, heads)
    width = out_ref.shape[1]
    start = pl.multiple_of((head % 2 ^ 1) * width, width)

    def work(i):
        out_ref[...] = product(attn, weights[i], start, width)

    for i in range(4):
        pl.when(node ^ i ^ (head // 2) == 3)(functools.partial(work, i))


def emit_kernel(counts, *refs):
    parts, weights, refs = unpack(counts, refs)
    outs, heads, terms = refs[:7], refs[7], refs[8]
    node, head = lax.axis_index("node"), lax.axis_index("head")
    far, near = head // 2, head % 2
    attn = gather_heads(parts, heads)
    width = outs[0].shape[1]
    for i in range(4):
        for side in range(2):
            start = pl.multiple_of((near ^ side) * width, width)
            terms[4 * side + (node ^ i ^ far)] = product(attn, weights[i], start, width)
    for i in range(7):
        outs[i][...] = terms[i]


def lead(parts, weights):
    rows = parts[0].shape[0]
    depth, cols = weights[0][0].shape
    counts = [len(pieces) for pieces in weights]
    return pl.pallas_call(
        functools.partial(lead_kernel, counts),
        out_shape=jax.ShapeDtypeStruct((rows, cols // 2), jnp.bfloat16),
        in_specs=[vmem_spec()] * (4 + sum(counts)),
        out_specs=vmem_spec(),
        scratch_shapes=[pltpu.VMEM((4, rows, DH), jnp.bfloat16)],
        compiler_params=pltpu.CompilerParams(vmem_limit_bytes=16 * 2**20),
        cost_estimate=pl.CostEstimate(
            flops=rows * depth * cols, bytes_accessed=depth * cols, transcendentals=0
        ),
        name="lead",
    )(*parts, *[piece for pieces in weights for piece in pieces])


def emit(parts, weights):
    rows = parts[0].shape[0]
    depth, cols = weights[0][0].shape
    counts = [len(pieces) for pieces in weights]
    flops = 2 * rows * depth * 4 * cols
    moved = 2 * (rows * depth + 4 * depth * cols + 4 * rows * cols)
    return pl.pallas_call(
        functools.partial(emit_kernel, counts),
        out_shape=[jax.ShapeDtypeStruct((rows, cols // 2), jnp.bfloat16)] * 7,
        in_specs=[vmem_spec()] * (4 + sum(counts)),
        out_specs=[vmem_spec()] * 7,
        scratch_shapes=[
            pltpu.VMEM((4, rows, DH), jnp.bfloat16),
            pltpu.VMEM((8, rows, cols // 2), jnp.bfloat16),
        ],
        compiler_params=pltpu.CompilerParams(vmem_limit_bytes=20 * 2**20),
        cost_estimate=pl.CostEstimate(flops=flops, bytes_accessed=moved, transcendentals=0),
        name="emit",
    )(*parts, *[piece for pieces in weights for piece in pieces])


def one_head_each(node_feats, w_qk, w_val, w_out, edge_types, rel_bias):
    depth, rows = w_out.shape[0], node_feats.shape[0]
    across = functools.partial(swap, axis="node", mask=2)
    beside = functools.partial(swap, axis="node", mask=1)
    along = functools.partial(swap, axis="head", mask=1)

    edges = [edge_types] + [swap(edge_types, "node", i) for i in range(1, 4)]
    far = {i: swap(node_feats, "head", 2 * i) for i in (3, 2, 1)}
    out_first = across(after(w_out[: depth // 2], *edges))
    edges = jnp.stack(edges)
    keep_0, send_0 = sort(node_feats, far[3], 1, 1)
    moved_0, keep_0y = [across(send_0[0])], [along(keep_0[0])]
    out_second = across(after(w_out[depth // 2 : 3 * depth // 4], moved_0[0], out_first))
    moved_0y = [along(moved_0[0])]
    close, distant = lax.optimization_barrier((far[1], far[2], keep_0y[0]))[:2]
    keep_1, send_1 = sort(close, distant, 1, 1)
    moved_1 = [across(part) for part in send_1]
    keep_1y = [along(keep_1[0])]
    moved_1y = [along(part) for part in moved_1]
    out_third = across(after(w_out[3 * depth // 4 :], moved_1[-1], out_second))
    qk_beside, val_beside = beside(w_qk), beside(w_val)
    qk_beside = after(qk_beside, out_first)
    pieces = [keep_0, keep_0y, keep_1, keep_1y, moved_0, moved_0y, moved_1, moved_1y]

    qk_keep, qk_send = project(pieces, [w_qk, qk_beside])
    qk_moved = across(qk_send)
    val_keep, val_send = project(pieces, [w_val, val_beside])
    val_moved = across(val_send)
    qk_mine, qk_give = combine(qk_keep, after(qk_moved, val_send, out_third))
    weights, total = weigh(edges, rel_bias.T, qk_mine, beside(qk_give))
    val_mine, val_give = combine(val_keep, after(val_moved, total))
    attn = average((0, 1, 2, 3), weights, total, val_mine, beside(val_give))
    attn = [attn[0]] + [swap(attn[i], "node", i) for i in range(1, 4)]

    out_across = [out_first, out_second, out_third]
    out_beside = beside(after(w_out, moved_1[0]))
    out_diagonal = [beside(after(piece, total)) for piece in out_across[:2]] + [beside(out_third)]
    first_send = lead(attn, [[w_out], [out_beside], out_across, out_diagonal])
    terms = emit(attn, [[w_out], [out_beside], out_across, out_diagonal])

    def pair(mine, send):
        return mine.astype(jnp.float32) + along(send).astype(jnp.float32)

    pair_3 = pair(terms[3], first_send).astype(jnp.bfloat16)
    pair_2 = pair(terms[2], terms[6]).astype(jnp.bfloat16)
    pair_1 = pair(terms[1], after(terms[5], pair_3)).astype(jnp.bfloat16)
    total = pair(terms[0], after(terms[4], pair_2))
    for i, part in ((3, pair_3), (2, pair_2), (1, pair_1)):
        total = total + swap(part, "head", 2 * i).astype(jnp.float32)
    return total.astype(jnp.bfloat16)


def from_behind(value, axis, by):
    peers = lax.axis_size(axis)
    return lax.ppermute(value, axis, [(i, (i + by) % peers) for i in range(peers)])


def pair_scores(queries, key_rows):
    inv_root = 1.0 / DH**0.5
    return (
        jnp.einsum("qhd,khd->hqk", queries, key_rows, preferred_element_type=jnp.float32) * inv_root
    )


def update(carried, scaled, bias_cols, value_rows, self_mask):
    head_count, query_count, key_count = scaled.shape
    tiles = bias_cols.shape[1]
    biased = (
        scaled.reshape(head_count, tiles, query_count // tiles, key_count)
        + bias_cols[:, :, None, :]
    )
    biased = biased.reshape(head_count, query_count, key_count)
    if self_mask is not None:
        biased = jnp.where(self_mask[None], NEG_BIG, biased)
    top_old, total_old, accum_old = carried
    top_new = jnp.maximum(top_old, jnp.max(biased, axis=2))
    expd = jnp.exp(biased - top_new[:, :, None])
    if self_mask is not None:
        expd = jnp.where(self_mask[None], 0.0, expd)
    factor = jnp.exp(top_old - top_new)
    total_new = total_old * factor + jnp.sum(expd, axis=2)
    product = jnp.einsum(
        "hqk,khd->hqd", expd.astype(jnp.bfloat16), value_rows, preferred_element_type=jnp.float32
    )
    return (top_new, total_new, accum_old * factor[:, :, None] + product)


def on_device(node_feats, w_qk, w_val, w_out, edge_types, rel_bias):
    row_count = node_feats.shape[0]
    col_width = w_qk.shape[1]
    head_count = rel_bias.shape[1]
    tile_rows = edge_types.shape[0]
    full_qk, full_val = (
        lax.all_gather(w_qk, "node", axis=0, tiled=True),
        lax.all_gather(w_val, "node", axis=0, tiled=True),
    )
    shard_piece = lax.all_gather(node_feats, "head", axis=1, tiled=True)
    proj_qk = jnp.dot(shard_piece, full_qk, preferred_element_type=jnp.float32)
    proj_val = jnp.dot(shard_piece, full_val, preferred_element_type=jnp.float32)
    qk_local = proj_qk.astype(jnp.bfloat16)
    val_local = proj_val.astype(jnp.bfloat16)
    queries = qk_local.reshape(row_count, head_count, DH)
    values = val_local.reshape(row_count, head_count, DH)
    relation_ids = jnp.arange(rel_bias.shape[0], dtype=jnp.int32)
    one_hot = (edge_types[:, :, None] == relation_ids[None, None, :]).astype(jnp.float32)
    tile_bias = jnp.einsum("abr,rh->hab", one_hot, rel_bias, precision=lax.Precision.HIGHEST)
    expanded = jnp.repeat(tile_bias, TILE, axis=2)
    my_block = lax.axis_index("node")
    first_row = my_block * row_count
    row_ids = first_row + jnp.arange(row_count, dtype=jnp.int32)
    initial = (
        jnp.full((head_count, row_count), NEG_BIG, jnp.float32),
        jnp.zeros((head_count, row_count), jnp.float32),
        jnp.zeros((head_count, row_count, DH), jnp.float32),
    )
    node_count = lax.axis_size("node")
    rounds = node_count // 2
    own_cols = lax.dynamic_slice_in_dim(expanded, first_row, row_count, 2)
    own_mask = row_ids[:, None] == row_ids[None, :]
    own_state = update(initial, pair_scores(queries, queries), own_cols, values, own_mask)

    def one_round(round_no, carried):
        mine, moving_block, moving_state = carried
        key_flat, value_flat = from_behind((moving_block[0], moving_block[1]), "node", 1)
        bias_moved, top_moved, total_moved, accum_moved = (
            from_behind(moving_state[0].astype(jnp.bfloat16), "node", 1).astype(jnp.float32),
            from_behind(moving_state[1].astype(jnp.bfloat16), "node", 1).astype(jnp.float32),
            from_behind(moving_state[2].astype(jnp.bfloat16), "node", 1).astype(jnp.float32),
            from_behind(moving_state[3].astype(jnp.bfloat16), "node", 1).astype(jnp.float32),
        )
        partner = (my_block - round_no) % node_count
        key_rows = key_flat.reshape(row_count, head_count, DH)
        value_rows = value_flat.reshape(row_count, head_count, DH)
        raw_scores = pair_scores(queries, key_rows)
        mine_cols = lax.dynamic_slice_in_dim(expanded, partner * row_count, row_count, 2)
        mine = update(mine, raw_scores, mine_cols, value_rows, None)
        back_tiles = lax.dynamic_slice_in_dim(bias_moved, my_block * tile_rows, tile_rows, 2)
        back_cols = jnp.repeat(back_tiles, TILE, axis=2)
        passed = update(
            (top_moved, total_moved, accum_moved),
            jnp.transpose(raw_scores, (0, 2, 1)),
            back_cols,
            values,
            None,
        )
        keep_flag = 2 * round_no != node_count
        kept = jax.tree.map(
            lambda fresh, stale: jnp.where(keep_flag, fresh, stale),
            passed,
            (top_moved, total_moved, accum_moved),
        )
        return (mine, (key_flat, value_flat), (bias_moved, kept[0], kept[1], kept[2]))

    start_state = (tile_bias, initial[0], initial[1], initial[2])
    own_state, _, final_moving = lax.fori_loop(
        1, rounds + 1, one_round, (own_state, (qk_local, val_local), start_state)
    )
    top_home, total_home, accum_home = (
        from_behind(final_moving[1].astype(jnp.bfloat16), "node", -rounds).astype(jnp.float32),
        from_behind(final_moving[2].astype(jnp.bfloat16), "node", -rounds).astype(jnp.float32),
        from_behind(final_moving[3].astype(jnp.bfloat16), "node", -rounds).astype(jnp.float32),
    )
    top_fin = jnp.maximum(own_state[0], top_home)
    factor_own = jnp.exp(own_state[0] - top_fin)
    factor_home = jnp.exp(top_home - top_fin)
    total_fin = own_state[1] * factor_own + total_home * factor_home
    accum_fin = own_state[2] * factor_own[:, :, None] + accum_home * factor_home[:, :, None]
    attn_heads = (accum_fin / total_fin[:, :, None]).astype(jnp.bfloat16)
    attn = jnp.transpose(attn_heads, (1, 0, 2)).reshape(row_count, col_width)
    terms = jnp.dot(
        attn, lax.all_gather(w_out, "node", axis=1, tiled=True), preferred_element_type=jnp.float32
    )
    return lax.psum_scatter(terms.astype(jnp.bfloat16), "head", scatter_dimension=1, tiled=True)

def solution(mesh):
    in_specs = (
        P("node", "head"),
        P("node", "head"),
        P("node", "head"),
        P("head", "node"),
        P("node", None),
        P(None, "head"),
    )
    out_specs = P("node", "head")

    def whole(node_feats, w_qk, w_val, w_out, edge_types, rel_bias):
        node_count, head_count = mesh.shape["node"], mesh.shape["head"]
        column_heads = rel_bias.shape[1] // head_count
        fits = (
            node_count == 4
            and head_count == 2 * node_count
            and column_heads == node_count
            and node_feats.shape[0] % (node_count * TILE) == 0
        )
        body = one_head_each if fits else on_device
        mapped = jax.shard_map(
            body, mesh=mesh, in_specs=in_specs, out_specs=out_specs, check_vma=False
        )
        return mapped(node_feats, w_qk, w_val, w_out, edge_types, rel_bias)

    return whole
```
